32 devices in a mesh: seq: 8 (over y, x, core), head: 4 (over z).
Axes of the slice: x: 2, y: 2, z: 4, core: 2. Of those that a mesh axis runs over, the one named last changes fastest.
Arguments:
- layer_input: bfloat16 [4096, 5376], P('seq'), may hold values from -6 to 6
- query: bfloat16 [4096, 4096], P('seq', 'head'), may hold values from -6 to 6
- keys: bfloat16 [4096, 2048], P('seq', 'head'), may hold values from -6 to 6
- values: bfloat16 [4096, 2048], P('seq', 'head'), may hold values from -6 to 6
- out_grad: bfloat16 [4096, 4096], P('seq', 'head'), may hold values from -6 to 6
- w_query: bfloat16 [5376, 4096], P(None, 'head'), may hold values from -0.078125 to 0.078125
- w_key: bfloat16 [5376, 2048], P(None, 'head'), may hold values from -0.078125 to 0.078125
- w_value: bfloat16 [5376, 2048], P(None, 'head'), may hold values from -0.078125 to 0.078125
- proof_lengths: int32 [8], replicated, may hold values from 1 to 2048, 4096 in all
Outputs:
- input_grad: bfloat16 [4096, 5376], P('seq', 'head')
- wq_grad: bfloat16 [5376, 4096], P('seq', 'head')
- wk_grad: bfloat16 [5376, 2048], P('seq', 'head')
- wv_grad: bfloat16 [5376, 2048], P('seq', 'head')
The draws below stay inside these ranges and needn't reach their ends.
Inputs may be any that keep to these rules, and one draw needn't show every extreme that they name: `proof_lengths`: the lengths of the 8 proofs packed in order; they sum to 4096 and the longest has exactly 2048 tokens.
All inputs are finite; a program needn't handle non-finite values.
Results may differ from the reference program's by a relative error of at most 0.015.
Values may be sent and summed in bfloat16 or wider, within the bound.
No kernel may reach another device: no remote copies, remote signals or barrier semaphores. Data moves between devices by JAX's collectives and lax.ppermute only.
A program may use at most 128 MiB of HBM per device.

```python
import math
import jax
import jax.numpy as jnp
import numpy as np
from jax import lax

D = 5376
H = 32
KV = 16
HD = 128
WINDOW = 1024
TOK_DEV = 512
TOKENS = 4096
PROOFS = 8
MOST_LEN = 2048
N_SEQ = 8
N_HEAD = 4


def drawn_pair(key):
    base_key = jax.random.fold_in(key, 7)
    parts_keys = jax.random.split(base_key, 2)
    query_out = jnp.clip(jax.random.normal(parts_keys[0], (TOKENS, H * HD), jnp.float32), -6.0, 6.0)
    key_out = jnp.clip(jax.random.normal(parts_keys[1], (TOKENS, KV * HD), jnp.float32), -6.0, 6.0)
    return (query_out, key_out)


def draw_query(key, part):
    return drawn_pair(key)[0].astype(jnp.bfloat16)


def draw_keys(key, part):
    return drawn_pair(key)[1].astype(jnp.bfloat16)


def raised(result, key, source, target, parts, factor):
    def block_of(position):
        return (jnp.arange(result.shape[position]) // (result.shape[position] // parts)).reshape((-1,) + (1,) * (result.ndim - 1 - position))

    near = jax.random.permutation(key, parts)[block_of(target)]
    far = (block_of(target) + parts // 2) % parts
    return jnp.where((block_of(source) == near) | (block_of(source) == far), factor * result, result)


def block_levels(rng, shape, pieces, smallest, top_value):
    level = 1.0
    for axis_at, parts in pieces:
        steps = jax.random.uniform(jax.random.fold_in(jax.random.fold_in(rng, 6), axis_at), (parts,), jnp.float32, smallest / len(pieces), top_value / len(pieces))
        level = level * jnp.repeat(jnp.exp(steps), shape[axis_at] // parts).reshape((-1,) + (1,) * (len(shape) - 1 - axis_at))
    return level


def split_up(count, total, reach, lean):
    weights = [(1 << 20) // math.isqrt(standing ** lean) + 1 for standing in range(2, count + 1)]
    surplus, holding = total - reach - (count - 1), [1] * (count - 1)
    while surplus > 0:
        candidates = [i for i in range(count - 1) if holding[i] < reach]
        mass, budget = sum([weights[i] for i in candidates]), surplus
        for i in candidates:
            extra = min(reach - holding[i], max(1, budget * weights[i] // mass), surplus)
            holding[i] = holding[i] + extra
            surplus = surplus - extra
    return np.array([reach] + holding)


def ragged(key, count, total, most, slope):
    if count == 2:
        one = jax.random.randint(key, (), max(1, total - most), min(most, total - 1) + 1)
        return jnp.stack([one, total - one])
    tallies = jnp.asarray(split_up(count, total, most, slope), jnp.int32)
    pairs = (count - 1) // 2
    source_of, sink = tallies[1:1 + 2 * pairs:2], tallies[2:2 + 2 * pairs:2]
    margin = jnp.minimum(source_of - 1, most - sink)
    moved = jax.random.randint(jax.random.fold_in(key, 1), (pairs,), 0, 1 << 20) % (margin + 1)
    tallies = tallies.at[1:1 + 2 * pairs:2].set(source_of - moved).at[2:2 + 2 * pairs:2].set(sink + moved)
    return tallies[jax.random.permutation(jax.random.fold_in(key, 2), count)]


def normal_values(own_key, extent, scale, limit, cuts=(), kind=jnp.bfloat16):
    values = scale * jax.random.normal(own_key, extent, jnp.float32)
    if cuts:
        values = values * block_levels(own_key, extent, cuts, -0.22, 0.18)
    return jnp.clip(values, -limit, limit).astype(kind)


def bell_draw_with(stream_key, shape, spread, most, shards, heavy, kind=jnp.bfloat16):
    entries = spread * jax.random.normal(stream_key, shape, jnp.float32)
    if shards:
        entries = entries * block_levels(stream_key, shape, shards, -0.22, 0.18)
    return jnp.clip(raised(entries, jax.random.fold_in(stream_key, 3), *heavy), -most, most).astype(kind)


def setup_inputs(seed: int = 0) -> dict:
    arg_keys = jax.random.split(jax.random.key(seed), 10)
    return {
        "layer_input": bell_draw_with(arg_keys[0], (TOKENS, D), 1.0, 6.0, ((0, 8),), (0, 1, 8, 2.0)),
        "query": draw_query(jax.random.fold_in(arg_keys[9], 71), 0),
        "keys": draw_keys(jax.random.fold_in(arg_keys[9], 71), 0),
        "values": normal_values(arg_keys[3], (TOKENS, KV * HD), 1.0, 6.0, ((0, 8), (1, 4))),
        "out_grad": normal_values(arg_keys[4], (TOKENS, H * HD), 1.0, 6.0, ((0, 8), (1, 4))),
        "w_query": normal_values(arg_keys[5], (D, H * HD), D ** -0.5, 0.078125, ((1, 4),)),
        "w_key": normal_values(arg_keys[6], (D, KV * HD), D ** -0.5, 0.078125, ((1, 4),)),
        "w_value": normal_values(arg_keys[7], (D, KV * HD), D ** -0.5, 0.078125, ((1, 4),)),
        "proof_lengths": ragged(arg_keys[8], PROOFS, TOKENS, MOST_LEN, 2).astype(jnp.int32),
    }


def proof_index(positions, proof_lengths):
    lengths_sum = jnp.cumsum(proof_lengths).astype(jnp.int32)
    starts_at = (lengths_sum - proof_lengths).astype(jnp.int32)
    counted = jnp.sum((positions[:, None] >= starts_at[None, :]).astype(jnp.int32), axis=1)
    return (counted - 1).astype(jnp.int32)


def build_mask(query_pos, key_pos, query_seg, key_seg):
    before = key_pos[None, :] <= query_pos[:, None]
    inside = query_pos[:, None] - key_pos[None, :] < WINDOW
    present = key_pos[None, :] >= 0
    same_proof = query_seg[:, None] == key_seg[None, :]
    return before & inside & present & same_proof


def rounded(value):
    return lax.optimization_barrier(value.astype(jnp.bfloat16)).astype(jnp.float32)


def block_grads(q_block, k_block, v_block, g_block, pair_mask, score_scale):
    scores = jnp.einsum("qkgd,lkd->kgql", q_block, k_block) * score_scale
    scores = jnp.where(pair_mask, scores, -1e30)
    row_max = jnp.max(scores, axis=-1, keepdims=True)
    weights_exp = jnp.where(pair_mask, jnp.exp(scores - row_max), 0.0)
    probs_full = weights_exp / jnp.sum(weights_exp, axis=-1, keepdims=True)
    probs_low = rounded(probs_full)
    attn_out = jnp.einsum("kgql,lkd->qkgd", probs_low, v_block)
    row_delta = jnp.einsum("qkgd,qkgd->kgq", g_block, attn_out)
    prob_grad = jnp.einsum("qkgd,lkd->kgql", g_block, v_block)
    score_low = rounded(probs_full * (prob_grad - row_delta[..., None]))
    query_grad = (score_scale * jnp.einsum("kgql,lkd->qkgd", score_low, k_block)).astype(jnp.bfloat16)
    key_grad = score_scale * jnp.einsum("kgql,qkgd->lkd", score_low, q_block)
    value_grad = jnp.einsum("kgql,qkgd->lkd", probs_low, g_block)
    return query_grad, key_grad, value_grad


def product_t(left, right):
    return jnp.dot(left.astype(jnp.float32), right.astype(jnp.float32).T, preferred_element_type=jnp.float32)


def reference(layer_input, query, keys, values, out_grad, w_query, w_key, w_value, proof_lengths):
    groups = H // KV
    score_scale = (D // H) ** -0.5
    block_rows = math.gcd(TOKENS, 512)
    span_rows = block_rows + WINDOW
    positions = jnp.arange(TOKENS, dtype=jnp.int32)
    segment_all = proof_index(positions, proof_lengths)
    padded_keys = jnp.concatenate([jnp.zeros((WINDOW, KV * HD), keys.dtype), keys], axis=0)
    padded_values = jnp.concatenate([jnp.zeros((WINDOW, KV * HD), values.dtype), values], axis=0)
    padded_segments = jnp.concatenate([jnp.full((WINDOW,), -1, jnp.int32), segment_all])

    def one_block(carry, block_index):
        key_acc, value_acc = carry
        first_row = (block_index * block_rows).astype(jnp.int32)
        q_block = lax.dynamic_slice_in_dim(query, first_row, block_rows, 0).astype(jnp.float32).reshape(block_rows, KV, groups, HD)
        g_block = lax.dynamic_slice_in_dim(out_grad, first_row, block_rows, 0).astype(jnp.float32).reshape(block_rows, KV, groups, HD)
        k_block = lax.dynamic_slice_in_dim(padded_keys, first_row, span_rows, 0).astype(jnp.float32).reshape(span_rows, KV, HD)
        v_block = lax.dynamic_slice_in_dim(padded_values, first_row, span_rows, 0).astype(jnp.float32).reshape(span_rows, KV, HD)
        query_pos = first_row + jnp.arange(block_rows, dtype=jnp.int32)
        key_pos = first_row - WINDOW + jnp.arange(span_rows, dtype=jnp.int32)
        query_seg = lax.dynamic_slice_in_dim(segment_all, first_row, block_rows, 0)
        key_seg = lax.dynamic_slice_in_dim(padded_segments, first_row, span_rows, 0)
        pair_mask = build_mask(query_pos, key_pos, query_seg, key_seg)
        q_grad, k_grad, v_grad = block_grads(q_block, k_block, v_block, g_block, pair_mask, score_scale)
        key_acc = lax.dynamic_update_slice_in_dim(key_acc, lax.dynamic_slice_in_dim(key_acc, first_row, span_rows, 0) + k_grad, first_row, 0)
        value_acc = lax.dynamic_update_slice_in_dim(value_acc, lax.dynamic_slice_in_dim(value_acc, first_row, span_rows, 0) + v_grad, first_row, 0)
        return (key_acc, value_acc), q_grad.reshape(block_rows, H * HD)

    start_acc = jnp.zeros((TOKENS + WINDOW, KV, HD), jnp.float32)
    block_ids = jnp.arange(TOKENS // block_rows, dtype=jnp.int32)
    (key_acc, value_acc), query_parts = lax.scan(one_block, (start_acc, start_acc), block_ids)
    query_grad = query_parts.reshape(TOKENS, H * HD)
    key_grad = key_acc[WINDOW:].reshape(TOKENS, KV * HD).astype(jnp.bfloat16)
    value_grad = value_acc[WINDOW:].reshape(TOKENS, KV * HD).astype(jnp.bfloat16)

    q_cols = H * HD // N_HEAD
    k_cols = KV * HD // N_HEAD
    input_sum = jnp.zeros((TOKENS, D), jnp.float32)
    for member in range(N_HEAD):
        q_lower = member * q_cols
        k_lower = member * k_cols
        head_term = product_t(query_grad[:, q_lower:q_lower + q_cols], w_query[:, q_lower:q_lower + q_cols])
        head_term = head_term + product_t(key_grad[:, k_lower:k_lower + k_cols], w_key[:, k_lower:k_lower + k_cols])
        head_term = head_term + product_t(value_grad[:, k_lower:k_lower + k_cols], w_value[:, k_lower:k_lower + k_cols])
        input_sum = input_sum + rounded(head_term)
    input_grad = input_sum.astype(jnp.bfloat16)

    all_grads = jnp.concatenate([query_grad, key_grad, value_grad], axis=1)

    def seq_term(carry, member):
        first_row = (member * TOK_DEV).astype(jnp.int32)
        inputs_part = lax.dynamic_slice_in_dim(layer_input, first_row, TOK_DEV, 0).astype(jnp.float32)
        grads_part = lax.dynamic_slice_in_dim(all_grads, first_row, TOK_DEV, 0).astype(jnp.float32)
        term = jnp.dot(inputs_part.T, grads_part, preferred_element_type=jnp.float32)
        return carry + rounded(term), None

    weight_total, _ = lax.scan(seq_term, jnp.zeros((D, (H + 2 * KV) * HD), jnp.float32), jnp.arange(N_SEQ, dtype=jnp.int32))
    wq_grad = weight_total[:, :H * HD].astype(jnp.bfloat16)
    wk_grad = weight_total[:, H * HD:H * HD + KV * HD].astype(jnp.bfloat16)
    wv_grad = weight_total[:, H * HD + KV * HD:].astype(jnp.bfloat16)
    return (input_grad, wq_grad, wk_grad, wv_grad)
```

```python
import functools
import math

import jax
import jax.numpy as jnp
from jax import lax
from jax.experimental import pallas as pl
from jax.experimental.pallas import tpu as pltpu
from jax.sharding import PartitionSpec as P

D = 5376
H = 32
HD = 128
WINDOW = 1024
TILE = 256
SCALE = (D // H) ** (-0.5)
FAR = -1e30
VMEM_BYTES = 56 * 1024 * 1024

NT = (((1,), (1,)), ((), ()))
TN = (((0,), (0,)), ((), ()))


def dot(left, right, dims=(((1,), (0,)), ((), ()))):
    return lax.dot_general(left, right, dims, preferred_element_type=jnp.float32)


def attention_kernel(groups, depth, lowest_ref, q_ref, g_ref, *refs):
    pieces = refs[: depth + 1]
    dq_ref = refs[depth + 1]
    halo_refs = refs[depth + 2 : 2 * depth + 2]
    own_ref = refs[2 * depth + 2]
    score_scr, pgrad_scr, dk_scr, dv_scr = refs[2 * depth + 3 :]
    rows = q_ref.shape[0]
    per_piece = rows // TILE
    behind = WINDOW // TILE
    lanes = groups * TILE

    def key_tile(e, which):
        start = (e % per_piece) * TILE
        return pieces[e // per_piece][which, start : start + TILE, :]

    key_iota = lax.broadcasted_iota(jnp.int32, (TILE, 1), 0)
    query_iota = lax.broadcasted_iota(jnp.int32, (1, TILE), 1)
    query_iota = jnp.concatenate([query_iota] * groups, axis=1)
    for t in range(per_piece):
        here = slice(t * TILE, (t + 1) * TILE)
        score_ref = score_scr.at[t % 2]
        pgrad_ref = pgrad_scr.at[t % 2]
        q2 = jnp.concatenate([q_ref[here, j * HD : (j + 1) * HD] for j in range(groups)], axis=0)
        g2 = jnp.concatenate([g_ref[here, j * HD : (j + 1) * HD] for j in range(groups)], axis=0)
        lowest = jnp.concatenate([lowest_ref[:, here]] * groups, axis=1)
        top = jnp.full((1, lanes), FAR, jnp.float32)
        for b in range(behind + 1):
            s = dot(key_tile(t + b, 0), q2, NT)
            allowed = key_iota + (t + b) * TILE >= lowest
            if b == behind:
                allowed = allowed & (key_iota <= query_iota)
            s = jnp.where(allowed, s, FAR)
            score_ref[b * TILE : (b + 1) * TILE, :] = s
            top = jnp.maximum(top, jnp.max(s, axis=0, keepdims=True))
        factor = SCALE * math.log2(math.e)
        total = jnp.zeros((1, lanes), jnp.float32)
        delta = jnp.zeros((1, lanes), jnp.float32)
        for b in range(behind + 1):
            at = slice(b * TILE, (b + 1) * TILE)
            weight = jnp.exp2((score_ref[at, :] - top) * factor)
            pgrad = dot(key_tile(t + b, 1), g2, NT)
            score_ref[at, :] = weight
            pgrad_ref[at, :] = pgrad
            total = total + jnp.sum(weight, axis=0, keepdims=True)
            delta = delta + jnp.sum(weight * pgrad, axis=0, keepdims=True)
        inverse = 1.0 / total
        delta = delta * inverse
        dq = jnp.zeros((HD, lanes), jnp.float32)
        for b in range(behind + 1):
            at = slice(b * TILE, (b + 1) * TILE)
            e = t + b
            to = slice(e * TILE, (e + 1) * TILE)
            prob = score_ref[at, :] * inverse
            sgrad = (prob * (pgrad_ref[at, :] - delta)).astype(jnp.bfloat16)
            dv = dot(prob.astype(jnp.bfloat16), g2)
            dk = dot(sgrad, q2)
            if t == 0 or b == behind:
                dv_scr[to, :] = dv
                dk_scr[to, :] = dk
            else:
                dv_scr[to, :] += dv
                dk_scr[to, :] += dk
            dq = dq + dot(key_tile(e, 0), sgrad, TN)
        dq = (dq * SCALE).T.astype(jnp.bfloat16)
        for j in range(groups):
            dq_ref[here, j * HD : (j + 1) * HD] = dq[j * TILE : (j + 1) * TILE, :]
    for d in range(depth):
        at = slice(d * rows, (d + 1) * rows)
        halo_refs[d][0] = (dk_scr[at, :] * SCALE).astype(jnp.bfloat16)
        halo_refs[d][1] = dv_scr[at, :].astype(jnp.bfloat16)
    own_ref[0] = dk_scr[depth * rows :, :] * SCALE
    own_ref[1] = dv_scr[depth * rows :, :]


def attention(lowest, query, out_grad, pieces, first, groups):
    rows = query.shape[0]
    depth = len(pieces) - 1
    heads = pieces[0].shape[2] // HD
    wide = groups * HD
    query_spec = pl.BlockSpec((rows, wide), lambda h: (0, h + first))
    pair_spec = pl.BlockSpec((2, rows, HD), lambda h: (0, 0, h))
    span = WINDOW + TILE
    pair = jax.ShapeDtypeStruct((2, rows, heads * HD), jnp.bfloat16)
    pairs_seen = heads * groups * rows * span
    return pl.pallas_call(
        functools.partial(attention_kernel, groups, depth),
        grid=(heads,),
        in_specs=[pl.BlockSpec((1, rows), lambda h: (0, 0)), query_spec, query_spec]
        + [pair_spec] * (depth + 1),
        out_specs=[pl.BlockSpec((rows, wide), lambda h: (0, h))] + [pair_spec] * (depth + 1),
        out_shape=[jax.ShapeDtypeStruct((rows, heads * wide), jnp.bfloat16)]
        + [pair] * depth
        + [jax.ShapeDtypeStruct(pair.shape, jnp.float32)],
        scratch_shapes=[
            pltpu.VMEM((2, span, groups * TILE), jnp.float32),
            pltpu.VMEM((2, span, groups * TILE), jnp.float32),
            pltpu.VMEM((WINDOW + rows, HD), jnp.float32),
            pltpu.VMEM((WINDOW + rows, HD), jnp.float32),
        ],
        compiler_params=pltpu.CompilerParams(vmem_limit_bytes=VMEM_BYTES),
        cost_estimate=pl.CostEstimate(
            flops=10 * pairs_seen * HD * 2,
            bytes_accessed=2 * rows * heads * HD * 20,
            transcendentals=pairs_seen,
        ),
        name="attention_grads",
    )(lowest, query, out_grad, *pieces)


def term_kernel(dq_ref, dk_ref, dv_ref, wq_ref, wk_ref, wv_ref, out_ref):
    out_ref[0] = (
        dot(dq_ref[...], wq_ref[...], NT)
        + dot(dk_ref[...], wk_ref[...], NT)
        + dot(dv_ref[...], wv_ref[...], NT)
    ).astype(jnp.bfloat16)


def input_term(dq, dk, dv, w_query, w_key, w_value, parts):
    rows = dq.shape[0]
    width = w_query.shape[0] // parts
    grads = [pl.BlockSpec(a.shape, lambda p: (0, 0)) for a in (dq, dk, dv)]
    weights = [pl.BlockSpec((width, w.shape[1]), lambda p: (p, 0)) for w in (w_query, w_key, w_value)]
    depth = dq.shape[1] + dk.shape[1] + dv.shape[1]
    return pl.pallas_call(
        term_kernel,
        grid=(parts,),
        in_specs=grads + weights,
        out_specs=pl.BlockSpec((1, rows, width), lambda p: (p, 0, 0)),
        out_shape=jax.ShapeDtypeStruct((parts, rows, width), jnp.bfloat16),
        compiler_params=pltpu.CompilerParams(vmem_limit_bytes=VMEM_BYTES),
        cost_estimate=pl.CostEstimate(
            flops=2 * rows * width * parts * depth,
            bytes_accessed=2 * (width * parts * (depth + rows) + rows * depth),
            transcendentals=0,
        ),
        name="input_term",
    )(dq, dk, dv, w_query, w_key, w_value)


def swapped(block, bit):
    size = lax.axis_size("seq")
    return lax.ppermute(block, "seq", [(i, i ^ bit) for i in range(size)])


def shifted(block, distance):
    size = lax.axis_size("seq")
    return lax.ppermute(
        block, "seq", [(i, i + distance) for i in range(size) if 0 <= i + distance < size]
    )


def earlier_pieces(own, odd):
    two_back = shifted(own, 2)
    one_back = swapped(jnp.where(odd, two_back, own), 1)
    return two_back, one_back


def returned(two_back, one_back, own, odd):
    beside = swapped(one_back, 1)
    both = two_back.astype(jnp.float32) + jnp.where(odd, beside.astype(jnp.float32), 0.0)
    later = shifted(both.astype(jnp.bfloat16), -2)
    total = own + later.astype(jnp.float32) + jnp.where(odd, 0.0, beside.astype(jnp.float32))
    return total.astype(jnp.bfloat16)


def scattered_product(rows_by_offset, grads, bits):
    size = len(rows_by_offset)
    arrived = {o: [] for o in range(size)}

    def summed(offset):
        value = dot(rows_by_offset[offset], grads)
        for other in arrived[offset]:
            value = value + other.astype(jnp.float32)
        return value.astype(jnp.bfloat16)

    alive = list(range(size))
    for bit in bits:
        leaving = [o for o in alive if o & bit]
        alive = [o for o in alive if not o & bit]
        for o in leaving:
            arrived[o ^ bit].append(swapped(summed(o), bit))
    return summed(0)


def on_device(layer_input, query, keys, values, out_grad, w_query, w_key, w_value, proof_lengths):
    rows = query.shape[0]
    key_cols = keys.shape[1]
    kv_local = key_cols // HD
    groups = query.shape[1] // key_cols
    seq_size = lax.axis_size("seq")
    head_size = lax.axis_size("head")
    me = lax.axis_index("seq")
    odd = me % 2 == 1
    first_row = me * rows

    positions = first_row + jnp.arange(rows, dtype=jnp.int32)
    starts = jnp.cumsum(proof_lengths) - proof_lengths
    begun = starts[:, None] <= positions[None, :]
    proof_start = jnp.max(jnp.where(begun, starts[:, None], 0), axis=0)
    lowest = jnp.maximum(proof_start, positions - (WINDOW - 1)) - first_row + WINDOW
    lowest = lowest.astype(jnp.int32)[None, :]

    sets = 2 if kv_local % 2 == 0 else 1
    per_set = kv_local // sets
    cols = per_set * HD
    dqs, dks, dvs = [], [], []
    stacked = []
    for c in range(sets):
        at = slice(c * cols, (c + 1) * cols)
        own = jnp.stack([keys[:, at], values[:, at]])
        stacked.append((earlier_pieces(own, odd), own))
    for c in range(sets):
        (two_back, one_back), own = stacked[c]
        dq, halo_two, halo_one, own_grad = attention(
            lowest, query, out_grad, [two_back, one_back, own], c * per_set, groups
        )
        total = returned(halo_two, halo_one, own_grad, odd)
        dqs.append(dq)
        dks.append(total[0])
        dvs.append(total[1])
    dq = jnp.concatenate(dqs, axis=1)
    dk = jnp.concatenate(dks, axis=1)
    dv = jnp.concatenate(dvs, axis=1)

    term = input_term(dq, dk, dv, w_query, w_key, w_value, head_size)
    input_grad = lax.psum_scatter(term, "head", scatter_dimension=0, tiled=False)

    block = layer_input.shape[1] // seq_size
    by_block = layer_input.T.reshape(seq_size, block, rows)
    order = me ^ jnp.arange(seq_size, dtype=jnp.int32)
    by_offset = [
        lax.dynamic_index_in_dim(by_block, order[o], 0, keepdims=False) for o in range(seq_size)
    ]
    bits = [1 << j for j in range(1, seq_size.bit_length() - 1)]
    forward = [1] + bits
    backward = [1] + bits[::-1]
    half = dq.shape[1] // 2
    wq_grad = jnp.concatenate(
        [
            scattered_product(by_offset, dq[:, :half], forward),
            scattered_product(by_offset, dq[:, half:], backward),
        ],
        axis=1,
    )
    wk_grad = scattered_product(by_offset, dk, forward)
    wv_grad = scattered_product(by_offset, dv, backward)
    return (input_grad, wq_grad, wk_grad, wv_grad)


def solution(mesh):
    return jax.shard_map(
        on_device,
        mesh=mesh,
        in_specs=(
            P("seq", None),
            P("seq", "head"),
            P("seq", "head"),
            P("seq", "head"),
            P("seq", "head"),
            P(None, "head"),
            P(None, "head"),
            P(None, "head"),
            P(),
        ),
        out_specs=(P("seq", "head"), P("seq", "head"), P("seq", "head"), P("seq", "head")),
        check_vma=False,
    )
```

```python
import functools
import math

import jax
import jax.numpy as jnp
from jax import lax
from jax.experimental import pallas as pl
from jax.experimental.pallas import tpu as pltpu
from jax.sharding import PartitionSpec as P

D = 5376
H = 32
HD = 128
WINDOW = 1024
TILE = 256
SCALE = (D // H) ** (-0.5)
FAR = -1e30
TOKEN_PARTS = 1
VMEM_BYTES = 56 * 1024 * 1024

NT = (((1,), (1,)), ((), ()))
TN = (((0,), (0,)), ((), ()))


def dot(left, right, dims=(((1,), (0,)), ((), ()))):
    return lax.dot_general(left, right, dims, preferred_element_type=jnp.float32)


def attention_kernel(groups, depth, lowest_ref, q_ref, g_ref, *refs):
    pieces = refs[: depth + 1]
    dq_ref = refs[depth + 1]
    halo_refs = refs[depth + 2 : 2 * depth + 2]
    own_ref = refs[2 * depth + 2]
    score_scr, pgrad_scr, dk_scr, dv_scr = refs[2 * depth + 3 :]
    rows = q_ref.shape[0]
    per_piece = rows // TILE
    behind = WINDOW // TILE
    lanes = groups * TILE

    def key_tile(e, which):
        start = (e % per_piece) * TILE
        return pieces[e // per_piece][which, start : start + TILE, :]

    key_iota = lax.broadcasted_iota(jnp.int32, (TILE, 1), 0)
    query_iota = lax.broadcasted_iota(jnp.int32, (1, TILE), 1)
    query_iota = jnp.concatenate([query_iota] * groups, axis=1)
    for t in range(per_piece):
        here = slice(t * TILE, (t + 1) * TILE)
        score_ref = score_scr.at[t % 2]
        pgrad_ref = pgrad_scr.at[t % 2]
        q2 = jnp.concatenate([q_ref[here, j * HD : (j + 1) * HD] for j in range(groups)], axis=0)
        g2 = jnp.concatenate([g_ref[here, j * HD : (j + 1) * HD] for j in range(groups)], axis=0)
        lowest = jnp.concatenate([lowest_ref[:, here]] * groups, axis=1)
        top = jnp.full((1, lanes), FAR, jnp.float32)
        for b in range(behind + 1):
            s = dot(key_tile(t + b, 0), q2, NT)
            allowed = key_iota + (t + b) * TILE >= lowest
            if b == behind:
                allowed = allowed & (key_iota <= query_iota)
            s = jnp.where(allowed, s, FAR)
            score_ref[b * TILE : (b + 1) * TILE, :] = s
            top = jnp.maximum(top, jnp.max(s, axis=0, keepdims=True))
        factor = SCALE * math.log2(math.e)
        total = jnp.zeros((1, lanes), jnp.float32)
        delta = jnp.zeros((1, lanes), jnp.float32)
        for b in range(behind + 1):
            at = slice(b * TILE, (b + 1) * TILE)
            weight = jnp.exp2((score_ref[at, :] - top) * factor)
            pgrad = dot(key_tile(t + b, 1), g2, NT)
            score_ref[at, :] = weight
            pgrad_ref[at, :] = pgrad
            total = total + jnp.sum(weight, axis=0, keepdims=True)
            delta = delta + jnp.sum(weight * pgrad, axis=0, keepdims=True)
        inverse = 1.0 / total
        delta = delta * inverse
        dq = jnp.zeros((HD, lanes), jnp.float32)
        for b in range(behind + 1):
            at = slice(b * TILE, (b + 1) * TILE)
            e = t + b
            to = slice(e * TILE, (e + 1) * TILE)
            prob = score_ref[at, :] * inverse
            sgrad = (prob * (pgrad_ref[at, :] - delta)).astype(jnp.bfloat16)
            dv = dot(prob.astype(jnp.bfloat16), g2)
            dk = dot(sgrad, q2)
            if t == 0 or b == behind:
                dv_scr[to, :] = dv
                dk_scr[to, :] = dk
            else:
                dv_scr[to, :] += dv
                dk_scr[to, :] += dk
            dq = dq + dot(key_tile(e, 0), sgrad, TN)
        dq = (dq * SCALE).T.astype(jnp.bfloat16)
        for j in range(groups):
            dq_ref[here, j * HD : (j + 1) * HD] = dq[j * TILE : (j + 1) * TILE, :]
    for d in range(depth):
        at = slice(d * rows, (d + 1) * rows)
        halo_refs[d][0] = (dk_scr[at, :] * SCALE).astype(jnp.bfloat16)
        halo_refs[d][1] = dv_scr[at, :].astype(jnp.bfloat16)
    own_ref[0] = dk_scr[depth * rows :, :] * SCALE
    own_ref[1] = dv_scr[depth * rows :, :]


def attention(lowest, query, out_grad, pieces, first, groups):
    rows = query.shape[0]
    depth = len(pieces) - 1
    heads = pieces[0].shape[2] // HD
    wide = groups * HD
    query_spec = pl.BlockSpec((rows, wide), lambda h: (0, h + first))
    pair_spec = pl.BlockSpec((2, rows, HD), lambda h: (0, 0, h))
    span = WINDOW + TILE
    pair = jax.ShapeDtypeStruct((2, rows, heads * HD), jnp.bfloat16)
    return pl.pallas_call(
        functools.partial(attention_kernel, groups, depth),
        grid=(heads,),
        in_specs=[pl.BlockSpec((1, rows), lambda h: (0, 0)), query_spec, query_spec]
        + [pair_spec] * (depth + 1),
        out_specs=[pl.BlockSpec((rows, wide), lambda h: (0, h))] + [pair_spec] * (depth + 1),
        out_shape=[jax.ShapeDtypeStruct((rows, heads * wide), jnp.bfloat16)]
        + [pair] * depth
        + [jax.ShapeDtypeStruct(pair.shape, jnp.float32)],
        scratch_shapes=[
            pltpu.VMEM((2, span, groups * TILE), jnp.float32),
            pltpu.VMEM((2, span, groups * TILE), jnp.float32),
            pltpu.VMEM((WINDOW + rows, HD), jnp.float32),
            pltpu.VMEM((WINDOW + rows, HD), jnp.float32),
        ],
        compiler_params=pltpu.CompilerParams(vmem_limit_bytes=VMEM_BYTES),
        name="attention_grads",
    )(lowest, query, out_grad, *pieces)


def arrange_kernel(order_ref, x_ref, first_ref, second_ref, scratch):
    width = first_ref.shape[1]
    step = pl.program_id(0)
    half = pl.num_programs(0) // 2

    @pl.when(step == 0)
    def _():
        tile = 768 if x_ref.shape[1] % 768 == 0 else 128
        for i in range(x_ref.shape[1] // tile):
            at = slice(i * tile, (i + 1) * tile)
            scratch[at, :] = x_ref[:, at].T

    start = pl.multiple_of(order_ref[step] * width, 16)

    @pl.when(step < half)
    def _():
        first_ref[0] = scratch[pl.ds(start, width), :]

    @pl.when(step >= half)
    def _():
        second_ref[0] = scratch[pl.ds(start, width), :]


def arranged(array, order, count):
    rows, cols = array.shape
    width, half = cols // count, count // 2
    out = jax.ShapeDtypeStruct((half, width, rows), array.dtype)
    return pl.pallas_call(
        arrange_kernel,
        grid_spec=pltpu.PrefetchScalarGridSpec(
            num_scalar_prefetch=1,
            grid=(count,),
            in_specs=[pl.BlockSpec((rows, cols), lambda i, order_ref: (0, 0))],
            out_specs=[
                pl.BlockSpec((1, width, rows), lambda i, order_ref: (jnp.minimum(i, half - 1), 0, 0)),
                pl.BlockSpec((1, width, rows), lambda i, order_ref: (jnp.maximum(i - half, 0), 0, 0)),
            ],
            scratch_shapes=[pltpu.VMEM((cols, rows), array.dtype)],
        ),
        out_shape=[out, out],
        compiler_params=pltpu.CompilerParams(vmem_limit_bytes=VMEM_BYTES),
        name="arranged_input",
    )(order, array)


def listed(values, index):
    total = jnp.int32(values[0])
    for i, value in enumerate(values[1:], 1):
        total = jnp.where(index == i, jnp.int32(value), total)
    return total


def paired_kernel(count, joined, *refs):
    outs = refs[2 * (2 + count) :]
    for side in range(2):
        x_ref, g_ref, *arrived = refs[side * (2 + count) : (side + 1) * (2 + count)]
        value = dot(x_ref[0], g_ref[...])
        for ref in arrived:
            value = value + ref[0].astype(jnp.float32)
        value = value.astype(jnp.bfloat16)
        if joined:
            cols = value.shape[1]
            outs[0][:, side * cols : (side + 1) * cols] = value
        else:
            outs[side][0] = value


def paired_products(sides, joined=False):
    specs, operands = [], []
    for inputs, grads, arrived, at in sides:
        for array, where in zip([inputs, *arrived], at):
            spec = pl.BlockSpec((1,) + array.shape[1:], lambda i, where=where: (listed(where, i), 0, 0))
            specs.append(spec)
            operands.append(array)
        place = len(specs) - len(arrived)
        specs.insert(place, pl.BlockSpec(grads.shape, lambda i: (0, 0)))
        operands.insert(place, grads)
    inputs, grads, arrived, at = sides[0]
    count, width, cols = len(at[0]), inputs.shape[1], grads.shape[1]
    if joined:
        out_specs = pl.BlockSpec((width, 2 * cols), lambda i: (0, 0))
        out_shape = jax.ShapeDtypeStruct((width, 2 * cols), jnp.bfloat16)
    else:
        out_specs = [pl.BlockSpec((1, width, cols), lambda i: (i, 0, 0))] * 2
        out_shape = [jax.ShapeDtypeStruct((count, width, cols), jnp.bfloat16)] * 2
    return pl.pallas_call(
        functools.partial(paired_kernel, len(arrived), joined),
        grid=(count,),
        in_specs=specs,
        out_specs=out_specs,
        out_shape=out_shape,
        compiler_params=pltpu.CompilerParams(vmem_limit_bytes=VMEM_BYTES),
        name="projection_products",
    )(*operands)


def term_kernel(dq_ref, dk_ref, dv_ref, wq_ref, wk_ref, wv_ref, out_ref):
    out_ref[0] = (
        dot(wq_ref[...], dq_ref[...], NT)
        + dot(wk_ref[...], dk_ref[...], NT)
        + dot(wv_ref[...], dv_ref[...], NT)
    ).astype(jnp.bfloat16)


def input_term(dq, dk, dv, w_query, w_key, w_value, parts, piece, pieces):
    rows = dq.shape[0] // pieces
    width = w_query.shape[0] // parts
    grads = [pl.BlockSpec((rows, a.shape[1]), lambda p: (piece, 0)) for a in (dq, dk, dv)]
    weights = [pl.BlockSpec((width, w.shape[1]), lambda p: (p, 0)) for w in (w_query, w_key, w_value)]
    return pl.pallas_call(
        term_kernel,
        grid=(parts,),
        in_specs=grads + weights,
        out_specs=pl.BlockSpec((1, width, rows), lambda p: (p, 0, 0)),
        out_shape=jax.ShapeDtypeStruct((parts, width, rows), jnp.bfloat16),
        compiler_params=pltpu.CompilerParams(vmem_limit_bytes=VMEM_BYTES),
        name="input_term",
    )(dq, dk, dv, w_query, w_key, w_value)


def swapped(block, bit):
    size = lax.axis_size("seq")
    return lax.ppermute(block, "seq", [(i, i ^ bit) for i in range(size)])


def shifted(block, distance):
    size = lax.axis_size("seq")
    return lax.ppermute(
        block, "seq", [(i, i + distance) for i in range(size) if 0 <= i + distance < size]
    )


def gray(index):
    return index ^ (index >> 1)


class Order:
    def __init__(self):
        self.last = ()

    def after(self, *values):
        values, _ = lax.optimization_barrier((values, self.last))
        return values if len(values) > 1 else values[0]

    def did(self, value):
        self.last = value
        return value


class Scattered:
    def __init__(self, inputs, offsets, grads, beside, bits):
        self.inputs, self.offsets, self.grads = inputs, offsets, list(grads)
        self.bits = [list(bits), list(bits[::-1])]
        self.alive = [list(offsets)] * 2
        self.arrived = [[(list(offsets), b)] for b in beside]

    def summed(self, order, leaving, joined=False):
        arrived = order.after(*[[array for _, array in held] for held in self.arrived])
        sides = []
        for i in range(2):
            at = [[held.index(o) for o in leaving[i]] for held, _ in self.arrived[i]]
            at.insert(0, [self.offsets.index(o) for o in leaving[i]])
            sides.append((self.inputs, self.grads[i], arrived[i], at))
        return order.did(paired_products(sides, joined))

    def step(self, order):
        bits = [b.pop(0) for b in self.bits]
        leaving = [[o for o in alive if o & bit] for alive, bit in zip(self.alive, bits)]
        self.alive = [[o for o in alive if not o & bit] for alive, bit in zip(self.alive, bits)]
        blocks = self.summed(order, leaving)
        for i in range(2):
            self.arrived[i].append(([o ^ bits[i] for o in leaving[i]], swapped(blocks[i], bits[i])))

    def result(self, order, joined=False):
        out = self.summed(order, [[0], [0]], joined)
        return out if joined else [o[0] for o in out]


def beside_products(odds, first, second):
    at = [list(range(odds.shape[0]))]
    blocks = paired_products([(odds, first, [], at), (odds, second, [], at)])
    return [swapped(block, 1) for block in blocks]


def kept_together(always, work, *operands):
    def nothing(*operands):
        return jax.tree.map(lambda a: jnp.zeros(a.shape, a.dtype), jax.eval_shape(work, *operands))

    return lax.cond(always, work, nothing, *operands)


def on_device(layer_input, query, keys, values, out_grad, w_query, w_key, w_value, proof_lengths):
    rows = query.shape[0]
    key_cols = keys.shape[1]
    kv_local = key_cols // HD
    groups = query.shape[1] // key_cols
    seq_size = lax.axis_size("seq")
    head_size = lax.axis_size("head")
    me = lax.axis_index("seq")
    odd = me % 2 == 1
    first_row = me * rows

    positions = first_row + jnp.arange(rows, dtype=jnp.int32)
    starts = jnp.cumsum(proof_lengths) - proof_lengths
    begun = starts[:, None] <= positions[None, :]
    proof_start = jnp.max(jnp.where(begun, starts[:, None], 0), axis=0)
    lowest = jnp.maximum(proof_start, positions - (WINDOW - 1)) - first_row + WINDOW
    lowest = lowest.astype(jnp.int32)[None, :]

    order = Order()
    sets = 2 if kv_local % 2 == 0 else 1
    per_set = kv_local // sets
    cols = per_set * HD

    def pair(c):
        at = slice(c * cols, (c + 1) * cols)
        return jnp.stack([keys[:, at], values[:, at]])

    own = order.did(pair(0))
    two_back = shifted(own, 2)
    steps = seq_size.bit_length() - 1
    even = [2 * gray(i) for i in range(1, seq_size // 2)] + [0]
    offsets = [o ^ 1 for o in even] + even
    layer_input = order.after(layer_input)
    odds, evens = order.did(arranged(layer_input, me ^ jnp.array(offsets, jnp.int32), seq_size))
    pieces = []
    for c in range(1, sets):
        keys, values = order.after(keys, values)
        other = order.did(pair(c))
        pieces.append([shifted(other, 2), shifted(other, 1), other])
    two_back = order.after(two_back)
    passed = order.did(jnp.where(odd, two_back, own))
    pieces.insert(0, [two_back, swapped(passed, 1), own])
    dqs, halos = [], []
    for c in range(sets):
        seen = order.after(*pieces[c])
        dq, halo_two, halo_one, own_grad = order.did(
            attention(lowest, query, out_grad, seen, c * per_set, groups)
        )
        dqs.append(dq)
        halos.append((own_grad, shifted(halo_one, -1), shifted(halo_two, -2)))
    dq = jnp.concatenate(dqs, axis=1)
    half = dq.shape[1] // 2
    if sets != 2:
        dqs = [dq[:, :half], dq[:, half:]]

    always = proof_lengths[0] > 0
    bits = [1 << j for j in range(1, steps)]
    totals = []
    for c, parts in enumerate(halos):
        if c == sets - 1:
            args = order.after(odds, *dqs)
            beside = order.did(kept_together(always, beside_products, *args))
        parts = order.after(*parts)
        total = sum(part.astype(jnp.float32) for part in parts).astype(jnp.bfloat16)
        totals.append(order.did(total))
    dk = jnp.concatenate([t[0] for t in totals], axis=1)
    dv = jnp.concatenate([t[1] for t in totals], axis=1)
    input_grads = []
    for i in range(TOKEN_PARTS):
        grads = order.after(dq, dk, dv)
        term = order.did(input_term(*grads, w_query, w_key, w_value, head_size, i, TOKEN_PARTS))
        input_grads.append(lax.psum_scatter(term, "head", scatter_dimension=0, tiled=False))
    input_grad = jnp.concatenate(input_grads, axis=1).T

    def projections(odds, evens, dqs, beside, dk, dv):
        order = Order()
        query_sum = Scattered(evens, even, dqs, beside, bits)
        query_sum.step(order)
        args = order.after(odds, dk, dv)
        beside = order.did(kept_together(always, beside_products, *args))
        other_sum = Scattered(evens, even, [dk, dv], beside, bits)
        other_sum.step(order)
        while query_sum.bits[0]:
            query_sum.step(order)
            other_sum.step(order)
        wq_grad = query_sum.result(order, True)
        return (wq_grad, *other_sum.result(order))

    parts = order.after(odds, evens, dqs, beside, dk, dv)
    grads = kept_together(always, projections, *parts)
    return (input_grad, *grads)


def solution(mesh):
    return jax.shard_map(
        on_device,
        mesh=mesh,
        in_specs=(
            P("seq", None),
            P("seq", "head"),
            P("seq", "head"),
            P("seq", "head"),
            P("seq", "head"),
            P(None, "head"),
            P(None, "head"),
            P(None, "head"),
            P(),
        ),
        out_specs=(P("seq", "head"), P("seq", "head"), P("seq", "head"), P("seq", "head")),
        check_vma=False,
    )
```

```python
import functools
import math

import jax
import jax.numpy as jnp
from jax import lax
from jax.experimental import pallas as pl
from jax.experimental.pallas import tpu as pltpu
from jax.sharding import PartitionSpec as P

D = 5376
H = 32
HD = 128
WINDOW = 1024
TILE = 256
SCALE = (D // H) ** (-0.5)
FAR = -1e30
VMEM_BYTES = 56 * 1024 * 1024

NT = (((1,), (1,)), ((), ()))
TN = (((0,), (0,)), ((), ()))


def dot(left, right, dims=(((1,), (0,)), ((), ()))):
    return lax.dot_general(left, right, dims, preferred_element_type=jnp.float32)


def attention_kernel(groups, depth, lowest_ref, q_ref, g_ref, *refs):
    pieces = refs[: depth + 1]
    dq_ref = refs[depth + 1]
    halo_refs = refs[depth + 2 : 2 * depth + 2]
    own_ref = refs[2 * depth + 2]
    score_scr, pgrad_scr, dk_scr, dv_scr = refs[2 * depth + 3 :]
    rows = q_ref.shape[0]
    per_piece = rows // TILE
    behind = WINDOW // TILE
    lanes = groups * TILE

    def key_tile(e, which):
        start = (e % per_piece) * TILE
        return pieces[e // per_piece][which, start : start + TILE, :]

    key_iota = lax.broadcasted_iota(jnp.int32, (TILE, 1), 0)
    query_iota = lax.broadcasted_iota(jnp.int32, (1, TILE), 1)
    query_iota = jnp.concatenate([query_iota] * groups, axis=1)
    for t in range(per_piece):
        here = slice(t * TILE, (t + 1) * TILE)
        score_ref = score_scr.at[t % 2]
        pgrad_ref = pgrad_scr.at[t % 2]
        q2 = jnp.concatenate([q_ref[here, j * HD : (j + 1) * HD] for j in range(groups)], axis=0)
        g2 = jnp.concatenate([g_ref[here, j * HD : (j + 1) * HD] for j in range(groups)], axis=0)
        lowest = jnp.concatenate([lowest_ref[:, here]] * groups, axis=1)
        top = jnp.full((1, lanes), FAR, jnp.float32)
        for b in range(behind + 1):
            s = dot(key_tile(t + b, 0), q2, NT)
            allowed = key_iota + (t + b) * TILE >= lowest
            if b == behind:
                allowed = allowed & (key_iota <= query_iota)
            s = jnp.where(allowed, s, FAR)
            score_ref[b * TILE : (b + 1) * TILE, :] = s
            top = jnp.maximum(top, jnp.max(s, axis=0, keepdims=True))
        factor = SCALE * math.log2(math.e)
        total = jnp.zeros((1, lanes), jnp.float32)
        delta = jnp.zeros((1, lanes), jnp.float32)
        for b in range(behind + 1):
            at = slice(b * TILE, (b + 1) * TILE)
            weight = jnp.exp2((score_ref[at, :] - top) * factor)
            pgrad = dot(key_tile(t + b, 1), g2, NT)
            score_ref[at, :] = weight
            pgrad_ref[at, :] = pgrad
            total = total + jnp.sum(weight, axis=0, keepdims=True)
            delta = delta + jnp.sum(weight * pgrad, axis=0, keepdims=True)
        inverse = 1.0 / total
        delta = delta * inverse
        dq = jnp.zeros((HD, lanes), jnp.float32)
        for b in range(behind + 1):
            at = slice(b * TILE, (b + 1) * TILE)
            e = t + b
            to = slice(e * TILE, (e + 1) * TILE)
            prob = score_ref[at, :] * inverse
            sgrad = (prob * (pgrad_ref[at, :] - delta)).astype(jnp.bfloat16)
            dv = dot(prob.astype(jnp.bfloat16), g2)
            dk = dot(sgrad, q2)
            if t == 0 or b == behind:
                dv_scr[to, :] = dv
                dk_scr[to, :] = dk
            else:
                dv_scr[to, :] += dv
                dk_scr[to, :] += dk
            dq = dq + dot(key_tile(e, 0), sgrad, TN)
        dq = (dq * SCALE).T.astype(jnp.bfloat16)
        for j in range(groups):
            dq_ref[here, j * HD : (j + 1) * HD] = dq[j * TILE : (j + 1) * TILE, :]
    for d in range(depth):
        at = slice(d * rows, (d + 1) * rows)
        halo_refs[d][0] = (dk_scr[at, :] * SCALE).astype(jnp.bfloat16)
        halo_refs[d][1] = dv_scr[at, :].astype(jnp.bfloat16)
    own_ref[0] = dk_scr[depth * rows :, :] * SCALE
    own_ref[1] = dv_scr[depth * rows :, :]


def attention(lowest, query, out_grad, pieces, first, groups):
    rows = query.shape[0]
    depth = len(pieces) - 1
    heads = pieces[0].shape[2] // HD
    wide = groups * HD
    query_spec = pl.BlockSpec((rows, wide), lambda h: (0, h + first))
    pair_spec = pl.BlockSpec((2, rows, HD), lambda h: (0, 0, h))
    span = WINDOW + TILE
    pair = jax.ShapeDtypeStruct((2, rows, heads * HD), jnp.bfloat16)
    return pl.pallas_call(
        functools.partial(attention_kernel, groups, depth),
        grid=(heads,),
        in_specs=[pl.BlockSpec((1, rows), lambda h: (0, 0)), query_spec, query_spec]
        + [pair_spec] * (depth + 1),
        out_specs=[pl.BlockSpec((rows, wide), lambda h: (0, h))] + [pair_spec] * (depth + 1),
        out_shape=[jax.ShapeDtypeStruct((rows, heads * wide), jnp.bfloat16)]
        + [pair] * depth
        + [jax.ShapeDtypeStruct(pair.shape, jnp.float32)],
        scratch_shapes=[
            pltpu.VMEM((2, span, groups * TILE), jnp.float32),
            pltpu.VMEM((2, span, groups * TILE), jnp.float32),
            pltpu.VMEM((WINDOW + rows, HD), jnp.float32),
            pltpu.VMEM((WINDOW + rows, HD), jnp.float32),
        ],
        compiler_params=pltpu.CompilerParams(vmem_limit_bytes=VMEM_BYTES),
        name="attention_grads",
    )(lowest, query, out_grad, *pieces)


def arrange_kernel(order_ref, x_ref, first_ref, second_ref, scratch):
    width = first_ref.shape[1]
    step = pl.program_id(0)
    half = pl.num_programs(0) // 2

    @pl.when(step == 0)
    def _():
        tile = 768 if x_ref.shape[1] % 768 == 0 else 128
        for i in range(x_ref.shape[1] // tile):
            at = slice(i * tile, (i + 1) * tile)
            scratch[at, :] = x_ref[:, at].T

    start = pl.multiple_of(order_ref[step] * width, 16)

    @pl.when(step < half)
    def _():
        first_ref[0] = scratch[pl.ds(start, width), :]

    @pl.when(step >= half)
    def _():
        second_ref[0] = scratch[pl.ds(start, width), :]


def arranged(array, order, count):
    rows, cols = array.shape
    width, half = cols // count, count // 2
    out = jax.ShapeDtypeStruct((half, width, rows), array.dtype)
    return pl.pallas_call(
        arrange_kernel,
        grid_spec=pltpu.PrefetchScalarGridSpec(
            num_scalar_prefetch=1,
            grid=(count,),
            in_specs=[pl.BlockSpec((rows, cols), lambda i, order_ref: (0, 0))],
            out_specs=[
                pl.BlockSpec((1, width, rows), lambda i, order_ref: (jnp.minimum(i, half - 1), 0, 0)),
                pl.BlockSpec((1, width, rows), lambda i, order_ref: (jnp.maximum(i - half, 0), 0, 0)),
            ],
            scratch_shapes=[pltpu.VMEM((cols, rows), array.dtype)],
        ),
        out_shape=[out, out],
        compiler_params=pltpu.CompilerParams(vmem_limit_bytes=VMEM_BYTES),
        name="arranged_input",
    )(order, array)


def listed(values, index):
    total = jnp.int32(values[0])
    for i, value in enumerate(values[1:], 1):
        total = jnp.where(index == i, jnp.int32(value), total)
    return total


def paired_kernel(count, joined, *refs):
    outs = refs[2 * (2 + count) :]
    for side in range(2):
        x_ref, g_ref, *arrived = refs[side * (2 + count) : (side + 1) * (2 + count)]
        value = dot(x_ref[0], g_ref[...])
        for ref in arrived:
            value = value + ref[0].astype(jnp.float32)
        value = value.astype(jnp.bfloat16)
        if joined:
            cols = value.shape[1]
            outs[0][:, side * cols : (side + 1) * cols] = value
        else:
            outs[side][0] = value


def paired_products(sides, joined=False):
    specs, operands = [], []
    for inputs, grads, arrived, at in sides:
        for array, where in zip([inputs, *arrived], at):
            spec = pl.BlockSpec((1,) + array.shape[1:], lambda i, where=where: (listed(where, i), 0, 0))
            specs.append(spec)
            operands.append(array)
        place = len(specs) - len(arrived)
        specs.insert(place, pl.BlockSpec(grads.shape, lambda i: (0, 0)))
        operands.insert(place, grads)
    inputs, grads, arrived, at = sides[0]
    count, width, cols = len(at[0]), inputs.shape[1], grads.shape[1]
    if joined:
        out_specs = pl.BlockSpec((width, 2 * cols), lambda i: (0, 0))
        out_shape = jax.ShapeDtypeStruct((width, 2 * cols), jnp.bfloat16)
    else:
        out_specs = [pl.BlockSpec((1, width, cols), lambda i: (i, 0, 0))] * 2
        out_shape = [jax.ShapeDtypeStruct((count, width, cols), jnp.bfloat16)] * 2
    return pl.pallas_call(
        functools.partial(paired_kernel, len(arrived), joined),
        grid=(count,),
        in_specs=specs,
        out_specs=out_specs,
        out_shape=out_shape,
        compiler_params=pltpu.CompilerParams(vmem_limit_bytes=VMEM_BYTES),
        name="projection_products",
    )(*operands)


def term_kernel(sets, *refs):
    dq_refs, refs = refs[:sets], refs[sets:]
    parts, refs = refs[: 3 * sets], refs[3 * sets :]
    wq_ref, wk_ref, wv_ref, out_ref, dk_ref, dv_ref = refs

    @pl.when(pl.program_id(0) == 0)
    def _():
        for c in range(sets):
            own_ref, one_ref, two_ref = parts[3 * c : 3 * c + 3]
            cols = own_ref.shape[2]
            at = slice(c * cols, (c + 1) * cols)
            for which, total_ref in enumerate((dk_ref, dv_ref)):
                total = own_ref[which] + one_ref[which].astype(jnp.float32)
                total = total + two_ref[which].astype(jnp.float32)
                total_ref[:, at] = total.astype(jnp.bfloat16)

    value = dot(wk_ref[...], dk_ref[...], NT) + dot(wv_ref[...], dv_ref[...], NT)
    for c, dq_ref in enumerate(dq_refs):
        cols = dq_ref.shape[1]
        value = value + dot(wq_ref[:, c * cols : (c + 1) * cols], dq_ref[...], NT)
    out_ref[0] = value.astype(jnp.bfloat16)


def input_term(dqs, halos, w_query, w_key, w_value, parts):
    sets, rows = len(dqs), dqs[0].shape[0]
    width = w_query.shape[0] // parts
    whole = [*dqs, *(part for halo in halos for part in halo)]
    weights = (w_query, w_key, w_value)
    key_cols = w_key.shape[1]

    def constant(array):
        return pl.BlockSpec(array.shape, lambda p: (0,) * array.ndim)

    total = jax.ShapeDtypeStruct((rows, key_cols), jnp.bfloat16)
    return pl.pallas_call(
        functools.partial(term_kernel, sets),
        grid=(parts,),
        in_specs=[constant(a) for a in whole]
        + [pl.BlockSpec((width, w.shape[1]), lambda p: (p, 0)) for w in weights],
        out_specs=[pl.BlockSpec((1, width, rows), lambda p: (p, 0, 0)), constant(total), constant(total)],
        out_shape=[jax.ShapeDtypeStruct((parts, width, rows), jnp.bfloat16), total, total],
        compiler_params=pltpu.CompilerParams(vmem_limit_bytes=VMEM_BYTES),
        name="input_term",
    )(*whole, *weights)


def swapped(block, bit):
    size = lax.axis_size("seq")
    return lax.ppermute(block, "seq", [(i, i ^ bit) for i in range(size)])


def shifted(block, distance):
    size = lax.axis_size("seq")
    return lax.ppermute(
        block, "seq", [(i, i + distance) for i in range(size) if 0 <= i + distance < size]
    )


def gray(index):
    return index ^ (index >> 1)


class Order:
    def __init__(self):
        self.last = ()

    def after(self, *values):
        values, _ = lax.optimization_barrier((values, self.last))
        return values if len(values) > 1 else values[0]

    def did(self, value):
        self.last = value
        return value


class Scattered:
    def __init__(self, offsets, bits):
        self.offsets = offsets
        self.bits = [list(bits), list(bits[::-1])]
        self.alive = [list(offsets)] * 2
        self.held = [[list(offsets)], [list(offsets)]]

    def summed(self, leaving, inputs, grads, arrived, joined=False):
        sides = []
        for i in range(2):
            at = [[held.index(o) for o in leaving[i]] for held in self.held[i]]
            at.insert(0, [self.offsets.index(o) for o in leaving[i]])
            sides.append((inputs, grads[i], [a[i] for a in arrived], at))
        return paired_products(sides, joined)

    def leaving(self, inputs, grads, arrived):
        leaving = [[o for o in self.alive[i] if o & self.bits[i][0]] for i in range(2)]
        return self.summed(leaving, inputs, grads, arrived)

    def step(self, blocks):
        bits = [b.pop(0) for b in self.bits]
        for i in range(2):
            self.held[i].append([o ^ bits[i] for o in self.alive[i] if o & bits[i]])
            self.alive[i] = [o for o in self.alive[i] if not o & bits[i]]
        return [swapped(block, bit) for block, bit in zip(blocks, bits)]

    def result(self, inputs, grads, arrived, joined=False):
        out = self.summed([[0], [0]], inputs, grads, arrived, joined)
        return out if joined else [o[0] for o in out]


def beside_products(odds, first, second):
    at = [list(range(odds.shape[0]))]
    blocks = paired_products([(odds, first, [], at), (odds, second, [], at)])
    return [swapped(block, 1) for block in blocks]


def kept_together(always, work, *operands):
    shapes = []

    def traced(*operands):
        out = work(*operands)
        shapes.append(jax.tree.map(lambda a: jax.ShapeDtypeStruct(a.shape, a.dtype), out))
        return out

    def nothing(*operands):
        return jax.tree.map(lambda a: jnp.zeros(a.shape, a.dtype), shapes[0])

    return lax.cond(always, traced, nothing, *operands)


def on_device(layer_input, query, keys, values, out_grad, w_query, w_key, w_value, proof_lengths):
    rows = query.shape[0]
    key_cols = keys.shape[1]
    kv_local = key_cols // HD
    groups = query.shape[1] // key_cols
    seq_size = lax.axis_size("seq")
    head_size = lax.axis_size("head")
    me = lax.axis_index("seq")
    odd = me % 2 == 1
    first_row = me * rows

    positions = first_row + jnp.arange(rows, dtype=jnp.int32)
    starts = jnp.cumsum(proof_lengths) - proof_lengths
    begun = starts[:, None] <= positions[None, :]
    proof_start = jnp.max(jnp.where(begun, starts[:, None], 0), axis=0)
    lowest = jnp.maximum(proof_start, positions - (WINDOW - 1)) - first_row + WINDOW
    lowest = lowest.astype(jnp.int32)[None, :]

    order = Order()
    sets = 2 if kv_local % 2 == 0 else 1
    per_set = kv_local // sets
    cols = per_set * HD

    def pair(c):
        at = slice(c * cols, (c + 1) * cols)
        return jnp.stack([keys[:, at], values[:, at]])

    own = order.did(pair(0))
    two_back = shifted(own, 2)
    steps = seq_size.bit_length() - 1
    even = [2 * gray(i) for i in range(1, seq_size // 2)] + [0]
    offsets = [o ^ 1 for o in even] + even
    layer_input = order.after(layer_input)
    odds, evens = order.did(arranged(layer_input, me ^ jnp.array(offsets, jnp.int32), seq_size))
    pieces = []
    for c in range(1, sets):
        keys, values = order.after(keys, values)
        other = order.did(pair(c))
        pieces.append([shifted(other, 2), shifted(other, 1), other])
    two_back = order.after(two_back)
    passed = order.did(jnp.where(odd, two_back, own))
    pieces.insert(0, [two_back, swapped(passed, 1), own])
    dqs, halos = [], []
    for c in range(sets):
        seen = order.after(*pieces[c])
        dq, halo_two, halo_one, own_grad = order.did(
            attention(lowest, query, out_grad, seen, c * per_set, groups)
        )
        dqs.append(dq)
        if c < sets - 1:
            halos.append((own_grad, shifted(halo_one, -1), shifted(halo_two, -2)))
    if sets == 2:
        halves = dqs
    else:
        half = dqs[0].shape[1] // 2
        halves = [dqs[0][:, :half], dqs[0][:, half:]]

    always = proof_lengths[0] > 0
    bits = [1 << j for j in range(1, steps)]
    query_sum, other_sum = Scattered(even, bits), Scattered(even, bits)

    def first_products(odds, evens, *dqs):
        beside = beside_products(odds, *dqs)
        return beside, query_sum.leaving(evens, dqs, [beside])

    def last_halo(halo_one, halo_two, *args):
        order = Order()
        arrived = shifted(halo_one, -1), shifted(halo_two, -2)
        products = order.did(kept_together(always, first_products, *args))
        return order.after(*arrived), products

    *args, early = order.after(halo_one, halo_two, odds, evens, *halves, [two for _, _, two in halos])
    halos = [(own, one, two) for (own, one, _), two in zip(halos, early)]
    arrived, (beside, blocks) = order.did(kept_together(always, last_halo, *args))
    halos.append((own_grad, *arrived))
    dqs, halos = order.after(dqs, halos)
    term, dk, dv = order.did(input_term(dqs, halos, w_query, w_key, w_value, head_size))

    def projections(odds, evens, dqs, beside, blocks, dk, dv):
        order = Order()
        arrived = [beside, query_sum.step(blocks)]
        args = order.after(odds, dk, dv)
        beside = order.did(kept_together(always, beside_products, *args))
        others = order.did(other_sum.leaving(evens, [dk, dv], [beside]))
        other_arrived = [beside, other_sum.step(others)]
        while query_sum.bits[0]:
            held = order.after(arrived)
            blocks = order.did(query_sum.leaving(evens, dqs, held))
            arrived = arrived + [query_sum.step(blocks)]
            held = order.after(other_arrived)
            blocks = order.did(other_sum.leaving(evens, [dk, dv], held))
            other_arrived = other_arrived + [other_sum.step(blocks)]
        held = order.after(arrived)
        wq_grad = order.did(query_sum.result(evens, dqs, held, True))
        held = order.after(other_arrived)
        return (wq_grad, *other_sum.result(evens, [dk, dv], held))

    def finish(term, *args):
        grads = kept_together(always, projections, *args)
        total = lax.psum_scatter(term, "head", scatter_dimension=0, tiled=False)
        return (total, *grads)

    args = order.after(odds, evens, halves, beside, blocks, dk, dv)
    input_grad, *grads = finish(term, *args)
    return (input_grad.T, *grads)


def solution(mesh):
    return jax.shard_map(
        on_device,
        mesh=mesh,
        in_specs=(
            P("seq", None),
            P("seq", "head"),
            P("seq", "head"),
            P("seq", "head"),
            P("seq", "head"),
            P(None, "head"),
            P(None, "head"),
            P(None, "head"),
            P(),
        ),
        out_specs=(P("seq", "head"), P("seq", "head"), P("seq", "head"), P("seq", "head")),
        check_vma=False,
    )
```

```python
import functools
import math

import jax
import jax.numpy as jnp
from jax import lax
from jax.experimental import pallas as pl
from jax.experimental.pallas import tpu as pltpu
from jax.sharding import PartitionSpec as P

D = 5376
H = 32
HD = 128
WINDOW = 1024
TILE = 256
SCALE = (D // H) ** (-0.5)
FAR = -1e30
VMEM_BYTES = 56 * 1024 * 1024

NT = (((1,), (1,)), ((), ()))
TN = (((0,), (0,)), ((), ()))


def dot(left, right, dims=(((1,), (0,)), ((), ()))):
    return lax.dot_general(left, right, dims, preferred_element_type=jnp.float32)


def attention_kernel(groups, depth, lowest_ref, q_ref, g_ref, *refs):
    pieces = refs[: depth + 1]
    dq_ref = refs[depth + 1]
    halo_refs = refs[depth + 2 : 2 * depth + 2]
    own_ref = refs[2 * depth + 2]
    score_scr, pgrad_scr, dk_scr, dv_scr = refs[2 * depth + 3 :]
    rows = q_ref.shape[0]
    per_piece = rows // TILE
    behind = WINDOW // TILE
    lanes = groups * TILE

    def key_tile(e, which):
        start = (e % per_piece) * TILE
        return pieces[e // per_piece][which, start : start + TILE, :]

    key_iota = lax.broadcasted_iota(jnp.int32, (TILE, 1), 0)
    query_iota = lax.broadcasted_iota(jnp.int32, (1, TILE), 1)
    query_iota = jnp.concatenate([query_iota] * groups, axis=1)
    factor = SCALE * math.log2(math.e)

    def scores(t):
        here = slice(t * TILE, (t + 1) * TILE)
        q2 = jnp.concatenate([q_ref[here, j * HD : (j + 1) * HD] for j in range(groups)], axis=0)
        g2 = jnp.concatenate([g_ref[here, j * HD : (j + 1) * HD] for j in range(groups)], axis=0)
        lowest = jnp.concatenate([lowest_ref[:, here]] * groups, axis=1)
        top = jnp.full((1, lanes), FAR, jnp.float32)
        for b in range(behind + 1):
            s = dot(key_tile(t + b, 0), q2, NT)
            allowed = key_iota + (t + b) * TILE >= lowest
            if b == behind:
                allowed = allowed & (key_iota <= query_iota)
            s = jnp.where(allowed, s, FAR)
            score_scr[t % 2, b * TILE : (b + 1) * TILE, :] = s
            top = jnp.maximum(top, jnp.max(s, axis=0, keepdims=True))
        return q2, g2, top

    def weights(t, q2, g2, top):
        total = jnp.zeros((1, lanes), jnp.float32)
        delta = jnp.zeros((1, lanes), jnp.float32)
        for b in range(behind + 1):
            at = slice(b * TILE, (b + 1) * TILE)
            weight = jnp.exp2((score_scr[t % 2, at, :] - top) * factor)
            pgrad = dot(key_tile(t + b, 1), g2, NT)
            score_scr[t % 2, at, :] = weight
            pgrad_scr[t % 2, at, :] = pgrad
            total = total + jnp.sum(weight, axis=0, keepdims=True)
            delta = delta + jnp.sum(weight * pgrad, axis=0, keepdims=True)
        inverse = 1.0 / total
        return q2, g2, inverse, delta * inverse

    def grads(t, q2, g2, inverse, delta):
        here = slice(t * TILE, (t + 1) * TILE)
        dq = jnp.zeros((HD, lanes), jnp.float32)
        for b in range(behind + 1):
            at = slice(b * TILE, (b + 1) * TILE)
            e = t + b
            to = slice(e * TILE, (e + 1) * TILE)
            prob = score_scr[t % 2, at, :] * inverse
            sgrad = (prob * (pgrad_scr[t % 2, at, :] - delta)).astype(jnp.bfloat16)
            dv = dot(prob.astype(jnp.bfloat16), g2)
            dk = dot(sgrad, q2)
            if t == 0 or b == behind:
                dv_scr[to, :] = dv
                dk_scr[to, :] = dk
            else:
                dv_scr[to, :] += dv
                dk_scr[to, :] += dk
            dq = dq + dot(key_tile(e, 0), sgrad, TN)
        dq = (dq * SCALE).T.astype(jnp.bfloat16)
        for j in range(groups):
            dq_ref[here, j * HD : (j + 1) * HD] = dq[j * TILE : (j + 1) * TILE, :]

    held = scores(0)
    for t in range(per_piece):
        held = weights(t, *held)
        later = scores(t + 1) if t + 1 < per_piece else None
        grads(t, *held)
        held = later
    for d in range(depth):
        at = slice(d * rows, (d + 1) * rows)
        halo_refs[d][0] = (dk_scr[at, :] * SCALE).astype(jnp.bfloat16)
        halo_refs[d][1] = dv_scr[at, :].astype(jnp.bfloat16)
    own_ref[0] = dk_scr[depth * rows :, :] * SCALE
    own_ref[1] = dv_scr[depth * rows :, :]


def attention(lowest, query, out_grad, pieces, first, groups):
    rows = query.shape[0]
    depth = len(pieces) - 1
    heads = pieces[0].shape[2] // HD
    wide = groups * HD
    query_spec = pl.BlockSpec((rows, wide), lambda h: (0, h + first))
    pair_spec = pl.BlockSpec((2, rows, HD), lambda h: (0, 0, h))
    span = WINDOW + TILE
    pair = jax.ShapeDtypeStruct((2, rows, heads * HD), jnp.bfloat16)
    return pl.pallas_call(
        functools.partial(attention_kernel, groups, depth),
        grid=(heads,),
        in_specs=[pl.BlockSpec((1, rows), lambda h: (0, 0)), query_spec, query_spec]
        + [pair_spec] * (depth + 1),
        out_specs=[pl.BlockSpec((rows, wide), lambda h: (0, h))] + [pair_spec] * (depth + 1),
        out_shape=[jax.ShapeDtypeStruct((rows, heads * wide), jnp.bfloat16)]
        + [pair] * depth
        + [jax.ShapeDtypeStruct(pair.shape, jnp.float32)],
        scratch_shapes=[
            pltpu.VMEM((2, span, groups * TILE), jnp.float32),
            pltpu.VMEM((2, span, groups * TILE), jnp.float32),
            pltpu.VMEM((WINDOW + rows, HD), jnp.float32),
            pltpu.VMEM((WINDOW + rows, HD), jnp.float32),
        ],
        compiler_params=pltpu.CompilerParams(vmem_limit_bytes=VMEM_BYTES),
        name="attention_grads",
    )(lowest, query, out_grad, *pieces)


def arrange_kernel(order_ref, x_ref, first_ref, second_ref, scratch):
    width = first_ref.shape[1]
    step = pl.program_id(0)
    half = pl.num_programs(0) // 2

    @pl.when(step == 0)
    def _():
        tile = 768 if x_ref.shape[1] % 768 == 0 else 128
        for i in range(x_ref.shape[1] // tile):
            at = slice(i * tile, (i + 1) * tile)
            scratch[at, :] = x_ref[:, at].T

    start = pl.multiple_of(order_ref[step] * width, 16)

    @pl.when(step < half)
    def _():
        first_ref[0] = scratch[pl.ds(start, width), :]

    @pl.when(step >= half)
    def _():
        second_ref[0] = scratch[pl.ds(start, width), :]


def arranged(array, order, count):
    rows, cols = array.shape
    width, half = cols // count, count // 2
    out = jax.ShapeDtypeStruct((half, width, rows), array.dtype)
    return pl.pallas_call(
        arrange_kernel,
        grid_spec=pltpu.PrefetchScalarGridSpec(
            num_scalar_prefetch=1,
            grid=(count,),
            in_specs=[pl.BlockSpec((rows, cols), lambda i, order_ref: (0, 0))],
            out_specs=[
                pl.BlockSpec((1, width, rows), lambda i, order_ref: (jnp.minimum(i, half - 1), 0, 0)),
                pl.BlockSpec((1, width, rows), lambda i, order_ref: (jnp.maximum(i - half, 0), 0, 0)),
            ],
            scratch_shapes=[pltpu.VMEM((cols, rows), array.dtype)],
        ),
        out_shape=[out, out],
        compiler_params=pltpu.CompilerParams(vmem_limit_bytes=VMEM_BYTES),
        name="arranged_input",
    )(order, array)


def listed(values, index):
    total = jnp.int32(values[0])
    for i, value in enumerate(values[1:], 1):
        total = jnp.where(index == i, jnp.int32(value), total)
    return total


def paired_kernel(count, joined, *refs):
    outs = refs[2 * (2 + count) :]
    for side in range(2):
        x_ref, g_ref, *arrived = refs[side * (2 + count) : (side + 1) * (2 + count)]
        value = dot(x_ref[0], g_ref[...])
        for ref in arrived:
            value = value + ref[0].astype(jnp.float32)
        value = value.astype(jnp.bfloat16)
        if joined:
            cols = value.shape[1]
            outs[0][:, side * cols : (side + 1) * cols] = value
        else:
            outs[side][0] = value


def paired_products(sides, joined=False):
    specs, operands = [], []
    for inputs, grads, arrived, at in sides:
        for array, where in zip([inputs, *arrived], at):
            spec = pl.BlockSpec((1,) + array.shape[1:], lambda i, where=where: (listed(where, i), 0, 0))
            specs.append(spec)
            operands.append(array)
        place = len(specs) - len(arrived)
        specs.insert(place, pl.BlockSpec(grads.shape, lambda i: (0, 0)))
        operands.insert(place, grads)
    inputs, grads, arrived, at = sides[0]
    count, width, cols = len(at[0]), inputs.shape[1], grads.shape[1]
    if joined:
        out_specs = pl.BlockSpec((width, 2 * cols), lambda i: (0, 0))
        out_shape = jax.ShapeDtypeStruct((width, 2 * cols), jnp.bfloat16)
    else:
        out_specs = [pl.BlockSpec((1, width, cols), lambda i: (i, 0, 0))] * 2
        out_shape = [jax.ShapeDtypeStruct((count, width, cols), jnp.bfloat16)] * 2
    return pl.pallas_call(
        functools.partial(paired_kernel, len(arrived), joined),
        grid=(count,),
        in_specs=specs,
        out_specs=out_specs,
        out_shape=out_shape,
        compiler_params=pltpu.CompilerParams(vmem_limit_bytes=VMEM_BYTES),
        name="projection_products",
    )(*operands)


def term_kernel(sets, *refs):
    dq_refs, refs = refs[:sets], refs[sets:]
    parts, refs = refs[: 3 * sets], refs[3 * sets :]
    wq_ref, wk_ref, wv_ref, out_ref, dk_ref, dv_ref = refs

    @pl.when(pl.program_id(0) == 0)
    def _():
        for c in range(sets):
            own_ref, one_ref, two_ref = parts[3 * c : 3 * c + 3]
            cols = own_ref.shape[2]
            at = slice(c * cols, (c + 1) * cols)
            for which, total_ref in enumerate((dk_ref, dv_ref)):
                total = own_ref[which] + one_ref[which].astype(jnp.float32)
                total = total + two_ref[which].astype(jnp.float32)
                total_ref[:, at] = total.astype(jnp.bfloat16)

    value = dot(wk_ref[...], dk_ref[...], NT) + dot(wv_ref[...], dv_ref[...], NT)
    for c, dq_ref in enumerate(dq_refs):
        cols = dq_ref.shape[1]
        value = value + dot(wq_ref[:, c * cols : (c + 1) * cols], dq_ref[...], NT)
    out_ref[0] = value.astype(jnp.bfloat16)


def input_term(dqs, halos, w_query, w_key, w_value, parts):
    sets, rows = len(dqs), dqs[0].shape[0]
    width = w_query.shape[0] // parts
    whole = [*dqs, *(part for halo in halos for part in halo)]
    weights = (w_query, w_key, w_value)
    key_cols = w_key.shape[1]

    def constant(array):
        return pl.BlockSpec(array.shape, lambda p: (0,) * array.ndim)

    total = jax.ShapeDtypeStruct((rows, key_cols), jnp.bfloat16)
    return pl.pallas_call(
        functools.partial(term_kernel, sets),
        grid=(parts,),
        in_specs=[constant(a) for a in whole]
        + [pl.BlockSpec((width, w.shape[1]), lambda p: (p, 0)) for w in weights],
        out_specs=[pl.BlockSpec((1, width, rows), lambda p: (p, 0, 0)), constant(total), constant(total)],
        out_shape=[jax.ShapeDtypeStruct((parts, width, rows), jnp.bfloat16), total, total],
        compiler_params=pltpu.CompilerParams(vmem_limit_bytes=VMEM_BYTES),
        name="input_term",
    )(*whole, *weights)


def swapped(block, bit):
    size = lax.axis_size("seq")
    return lax.ppermute(block, "seq", [(i, i ^ bit) for i in range(size)])


def shifted(block, distance):
    size = lax.axis_size("seq")
    return lax.ppermute(
        block, "seq", [(i, i + distance) for i in range(size) if 0 <= i + distance < size]
    )


def gray(index):
    return index ^ (index >> 1)


class Order:
    def __init__(self):
        self.last = ()

    def after(self, *values):
        values, _ = lax.optimization_barrier((values, self.last))
        return values if len(values) > 1 else values[0]

    def did(self, value):
        self.last = value
        return value


class Scattered:
    def __init__(self, offsets, bits):
        self.offsets = offsets
        self.bits = [list(bits), list(bits[::-1])]
        self.alive = [list(offsets)] * 2
        self.held = [[list(offsets)], [list(offsets)]]

    def summed(self, leaving, inputs, grads, arrived, joined=False):
        sides = []
        for i in range(2):
            at = [[held.index(o) for o in leaving[i]] for held in self.held[i]]
            at.insert(0, [self.offsets.index(o) for o in leaving[i]])
            sides.append((inputs, grads[i], [a[i] for a in arrived], at))
        return paired_products(sides, joined)

    def leaving(self, inputs, grads, arrived):
        leaving = [[o for o in self.alive[i] if o & self.bits[i][0]] for i in range(2)]
        return self.summed(leaving, inputs, grads, arrived)

    def step(self, blocks):
        bits = [b.pop(0) for b in self.bits]
        for i in range(2):
            self.held[i].append([o ^ bits[i] for o in self.alive[i] if o & bits[i]])
            self.alive[i] = [o for o in self.alive[i] if not o & bits[i]]
        return [swapped(block, bit) for block, bit in zip(blocks, bits)]

    def result(self, inputs, grads, arrived, joined=False):
        out = self.summed([[0], [0]], inputs, grads, arrived, joined)
        return out if joined else [o[0] for o in out]


def beside_products(odds, first, second):
    at = [list(range(odds.shape[0]))]
    blocks = paired_products([(odds, first, [], at), (odds, second, [], at)])
    return [swapped(block, 1) for block in blocks]


def kept_together(always, work, *operands):
    shapes = []

    def traced(*operands):
        out = work(*operands)
        shapes.append(jax.tree.map(lambda a: jax.ShapeDtypeStruct(a.shape, a.dtype), out))
        return out

    def nothing(*operands):
        return jax.tree.map(lambda a: jnp.zeros(a.shape, a.dtype), shapes[0])

    return lax.cond(always, traced, nothing, *operands)


def on_device(layer_input, query, keys, values, out_grad, w_query, w_key, w_value, proof_lengths):
    rows = query.shape[0]
    key_cols = keys.shape[1]
    kv_local = key_cols // HD
    groups = query.shape[1] // key_cols
    seq_size = lax.axis_size("seq")
    head_size = lax.axis_size("head")
    me = lax.axis_index("seq")
    odd = me % 2 == 1
    first_row = me * rows

    positions = first_row + jnp.arange(rows, dtype=jnp.int32)
    starts = jnp.cumsum(proof_lengths) - proof_lengths
    begun = starts[:, None] <= positions[None, :]
    proof_start = jnp.max(jnp.where(begun, starts[:, None], 0), axis=0)
    lowest = jnp.maximum(proof_start, positions - (WINDOW - 1)) - first_row + WINDOW
    lowest = lowest.astype(jnp.int32)[None, :]

    order = Order()
    sets = 2 if kv_local % 2 == 0 else 1
    per_set = kv_local // sets
    cols = per_set * HD

    def pair(c):
        at = slice(c * cols, (c + 1) * cols)
        return jnp.stack([keys[:, at], values[:, at]])

    own = order.did(pair(0))
    two_back = shifted(own, 2)
    steps = seq_size.bit_length() - 1
    even = [2 * gray(i) for i in range(1, seq_size // 2)] + [0]
    offsets = [o ^ 1 for o in even] + even
    layer_input = order.after(layer_input)
    odds, evens = order.did(arranged(layer_input, me ^ jnp.array(offsets, jnp.int32), seq_size))
    pieces = []
    for c in range(1, sets):
        keys, values = order.after(keys, values)
        other = order.did(pair(c))
        pieces.append([shifted(other, 2), shifted(other, 1), other])
    two_back = order.after(two_back)
    passed = order.did(jnp.where(odd, two_back, own))
    pieces.insert(0, [two_back, swapped(passed, 1), own])
    dqs, halos = [], []
    for c in range(sets):
        seen = order.after(*pieces[c])
        dq, halo_two, halo_one, own_grad = order.did(
            attention(lowest, query, out_grad, seen, c * per_set, groups)
        )
        dqs.append(dq)
        if c < sets - 1:
            halos.append((own_grad, shifted(halo_one, -1), shifted(halo_two, -2)))
    if sets == 2:
        halves = dqs
    else:
        half = dqs[0].shape[1] // 2
        halves = [dqs[0][:, :half], dqs[0][:, half:]]

    always = proof_lengths[0] > 0
    bits = [1 << j for j in range(1, steps)]
    query_sum, other_sum = Scattered(even, bits), Scattered(even, bits)

    def first_products(odds, evens, *dqs):
        beside = beside_products(odds, *dqs)
        return beside, query_sum.leaving(evens, dqs, [beside])

    def last_halo(halo_one, halo_two, *args):
        order = Order()
        arrived = shifted(halo_one, -1), shifted(halo_two, -2)
        products = order.did(kept_together(always, first_products, *args))
        return order.after(*arrived), products

    *args, early = order.after(halo_one, halo_two, odds, evens, *halves, [two for _, _, two in halos])
    halos = [(own, one, two) for (own, one, _), two in zip(halos, early)]
    arrived, (beside, blocks) = order.did(kept_together(always, last_halo, *args))
    halos.append((own_grad, *arrived))
    dqs, halos = order.after(dqs, halos)
    term, dk, dv = order.did(input_term(dqs, halos, w_query, w_key, w_value, head_size))

    def projections(odds, evens, dqs, beside, blocks, dk, dv):
        order = Order()
        arrived = [beside, query_sum.step(blocks)]
        args = order.after(odds, dk, dv)
        beside = order.did(kept_together(always, beside_products, *args))
        others = order.did(other_sum.leaving(evens, [dk, dv], [beside]))
        other_arrived = [beside, other_sum.step(others)]
        while query_sum.bits[0]:
            held = order.after(arrived)
            blocks = order.did(query_sum.leaving(evens, dqs, held))
            arrived = arrived + [query_sum.step(blocks)]
            held = order.after(other_arrived)
            blocks = order.did(other_sum.leaving(evens, [dk, dv], held))
            other_arrived = other_arrived + [other_sum.step(blocks)]
        held = order.after(arrived)
        wq_grad = order.did(query_sum.result(evens, dqs, held, True))
        held = order.after(other_arrived)
        return (wq_grad, *other_sum.result(evens, [dk, dv], held))

    def finish(term, *args):
        grads = kept_together(always, projections, *args)
        total = lax.psum_scatter(term, "head", scatter_dimension=0, tiled=False)
        return (total, *grads)

    args = order.after(odds, evens, halves, beside, blocks, dk, dv)
    input_grad, *grads = finish(term, *args)
    return (input_grad.T, *grads)


def solution(mesh):
    return jax.shard_map(
        on_device,
        mesh=mesh,
        in_specs=(
            P("seq", None),
            P("seq", "head"),
            P("seq", "head"),
            P("seq", "head"),
            P("seq", "head"),
            P(None, "head"),
            P(None, "head"),
            P(None, "head"),
            P(),
        ),
        out_specs=(P("seq", "head"), P("seq", "head"), P("seq", "head"), P("seq", "head")),
        check_vma=False,
    )
```

```python
import functools
import math

import jax
import jax.numpy as jnp
from jax import lax
from jax.experimental import pallas as pl
from jax.experimental.pallas import tpu as pltpu
from jax.sharding import PartitionSpec as P

D = 5376
H = 32
HD = 128
WINDOW = 1024
TILE = 256
SCALE = (D // H) ** (-0.5)
FAR = -1e30
VMEM_BYTES = 56 * 1024 * 1024

NT = (((1,), (1,)), ((), ()))
TN = (((0,), (0,)), ((), ()))


def dot(left, right, dims=(((1,), (0,)), ((), ()))):
    return lax.dot_general(left, right, dims, preferred_element_type=jnp.float32)


def attention_kernel(groups, depth, lowest_ref, q_ref, g_ref, *refs):
    pieces = refs[: depth + 1]
    dq_ref = refs[depth + 1]
    halo_refs = refs[depth + 2 : 2 * depth + 2]
    own_ref = refs[2 * depth + 2]
    score_scr, pgrad_scr, dk_scr, dv_scr = refs[2 * depth + 3 :]
    rows = q_ref.shape[0]
    per_piece = rows // TILE
    behind = WINDOW // TILE
    lanes = groups * TILE

    def key_tile(e, which):
        start = (e % per_piece) * TILE
        return pieces[e // per_piece][which, start : start + TILE, :]

    key_iota = lax.broadcasted_iota(jnp.int32, (TILE, 1), 0)
    query_iota = lax.broadcasted_iota(jnp.int32, (1, TILE), 1)
    query_iota = jnp.concatenate([query_iota] * groups, axis=1)
    factor = SCALE * math.log2(math.e)

    def scores(t):
        here = slice(t * TILE, (t + 1) * TILE)
        q2 = jnp.concatenate([q_ref[here, j * HD : (j + 1) * HD] for j in range(groups)], axis=0)
        g2 = jnp.concatenate([g_ref[here, j * HD : (j + 1) * HD] for j in range(groups)], axis=0)
        lowest = jnp.concatenate([lowest_ref[:, here]] * groups, axis=1)
        top = jnp.full((1, lanes), FAR, jnp.float32)
        for b in range(behind + 1):
            s = dot(key_tile(t + b, 0), q2, NT)
            allowed = key_iota + (t + b) * TILE >= lowest
            if b == behind:
                allowed = allowed & (key_iota <= query_iota)
            s = jnp.where(allowed, s, FAR)
            score_scr[t % 2, b * TILE : (b + 1) * TILE, :] = s
            top = jnp.maximum(top, jnp.max(s, axis=0, keepdims=True))
        return q2, g2, top

    def weights(t, q2, g2, top):
        total = jnp.zeros((1, lanes), jnp.float32)
        delta = jnp.zeros((1, lanes), jnp.float32)
        for b in range(behind + 1):
            at = slice(b * TILE, (b + 1) * TILE)
            weight = jnp.exp2((score_scr[t % 2, at, :] - top) * factor)
            pgrad = dot(key_tile(t + b, 1), g2, NT)
            score_scr[t % 2, at, :] = weight
            pgrad_scr[t % 2, at, :] = pgrad
            total = total + jnp.sum(weight, axis=0, keepdims=True)
            delta = delta + jnp.sum(weight * pgrad, axis=0, keepdims=True)
        inverse = 1.0 / total
        return q2, g2, inverse, delta * inverse

    def grads(t, q2, g2, inverse, delta):
        here = slice(t * TILE, (t + 1) * TILE)
        dq = jnp.zeros((HD, lanes), jnp.float32)
        for b in range(behind + 1):
            at = slice(b * TILE, (b + 1) * TILE)
            e = t + b
            to = slice(e * TILE, (e + 1) * TILE)
            prob = score_scr[t % 2, at, :] * inverse
            sgrad = (prob * (pgrad_scr[t % 2, at, :] - delta)).astype(jnp.bfloat16)
            dv = dot(prob.astype(jnp.bfloat16), g2)
            dk = dot(sgrad, q2)
            if t == 0 or b == behind:
                dv_scr[to, :] = dv
                dk_scr[to, :] = dk
            else:
                dv_scr[to, :] += dv
                dk_scr[to, :] += dk
            dq = dq + dot(key_tile(e, 0), sgrad, TN)
        dq = (dq * SCALE).T.astype(jnp.bfloat16)
        for j in range(groups):
            dq_ref[here, j * HD : (j + 1) * HD] = dq[j * TILE : (j + 1) * TILE, :]

    held = scores(0)
    for t in range(per_piece):
        held = weights(t, *held)
        later = scores(t + 1) if t + 1 < per_piece else None
        grads(t, *held)
        held = later
    for d in range(depth):
        at = slice(d * rows, (d + 1) * rows)
        halo_refs[d][0] = (dk_scr[at, :] * SCALE).astype(jnp.bfloat16)
        halo_refs[d][1] = dv_scr[at, :].astype(jnp.bfloat16)
    own_ref[0] = dk_scr[depth * rows :, :] * SCALE
    own_ref[1] = dv_scr[depth * rows :, :]


def attention(lowest, query, out_grad, pieces, first, groups):
    rows = query.shape[0]
    depth = len(pieces) - 1
    heads = pieces[0].shape[2] // HD
    wide = groups * HD
    query_spec = pl.BlockSpec((rows, wide), lambda h: (0, h + first))
    pair_spec = pl.BlockSpec((2, rows, HD), lambda h: (0, 0, h))
    span = WINDOW + TILE
    pair = jax.ShapeDtypeStruct((2, rows, heads * HD), jnp.bfloat16)
    return pl.pallas_call(
        functools.partial(attention_kernel, groups, depth),
        grid=(heads,),
        in_specs=[pl.BlockSpec((1, rows), lambda h: (0, 0)), query_spec, query_spec]
        + [pair_spec] * (depth + 1),
        out_specs=[pl.BlockSpec((rows, wide), lambda h: (0, h))] + [pair_spec] * (depth + 1),
        out_shape=[jax.ShapeDtypeStruct((rows, heads * wide), jnp.bfloat16)]
        + [pair] * depth
        + [jax.ShapeDtypeStruct(pair.shape, jnp.float32)],
        scratch_shapes=[
            pltpu.VMEM((2, span, groups * TILE), jnp.float32),
            pltpu.VMEM((2, span, groups * TILE), jnp.float32),
            pltpu.VMEM((WINDOW + rows, HD), jnp.float32),
            pltpu.VMEM((WINDOW + rows, HD), jnp.float32),
        ],
        compiler_params=pltpu.CompilerParams(vmem_limit_bytes=VMEM_BYTES),
        name="attention_grads",
    )(lowest, query, out_grad, *pieces)


def arrange_kernel(offsets, me_ref, x_ref, first_ref, second_ref, scratch):
    width = first_ref.shape[1]
    step = pl.program_id(0)
    half = pl.num_programs(0) // 2

    @pl.when(step == 0)
    def _():
        tile = 768 if x_ref.shape[1] % 768 == 0 else 128
        for i in range(x_ref.shape[1] // tile):
            at = slice(i * tile, (i + 1) * tile)
            scratch[at, :] = x_ref[:, at].T

    start = pl.multiple_of((listed(offsets, step) ^ me_ref[0]) * width, 16)

    @pl.when(step < half)
    def _():
        first_ref[0] = scratch[pl.ds(start, width), :]

    @pl.when(step >= half)
    def _():
        second_ref[0] = scratch[pl.ds(start, width), :]


def arranged(array, me, offsets):
    rows, cols = array.shape
    count = len(offsets)
    width, half = cols // count, count // 2
    out = jax.ShapeDtypeStruct((half, width, rows), array.dtype)
    return pl.pallas_call(
        functools.partial(arrange_kernel, offsets),
        grid_spec=pltpu.PrefetchScalarGridSpec(
            num_scalar_prefetch=1,
            grid=(count,),
            in_specs=[pl.BlockSpec((rows, cols), lambda i, me_ref: (0, 0))],
            out_specs=[
                pl.BlockSpec((1, width, rows), lambda i, me_ref: (jnp.minimum(i, half - 1), 0, 0)),
                pl.BlockSpec((1, width, rows), lambda i, me_ref: (jnp.maximum(i - half, 0), 0, 0)),
            ],
            scratch_shapes=[pltpu.VMEM((cols, rows), array.dtype)],
        ),
        out_shape=[out, out],
        compiler_params=pltpu.CompilerParams(vmem_limit_bytes=VMEM_BYTES),
        name="arranged_input",
    )(me.reshape(1), array)


def listed(values, index):
    total = jnp.int32(values[0])
    for i, value in enumerate(values[1:], 1):
        total = jnp.where(index == i, jnp.int32(value), total)
    return total


def paired_kernel(count, shared, joined, *refs):
    sides = 2 * [refs[:1]] if shared else [refs[:1], refs[2 + count : 3 + count]]
    sides = [(*x, *refs[i * (1 + count) + (1 if shared else i + 1) :][: 1 + count]) for i, x in enumerate(sides)]
    outs = refs[2 * (1 + count) + (1 if shared else 2) :]
    for side in range(2):
        x_ref, g_ref, *arrived = sides[side]
        value = dot(x_ref[0], g_ref[...])
        for ref in arrived:
            value = value + ref[0].astype(jnp.float32)
        value = value.astype(jnp.bfloat16)
        if joined:
            cols = value.shape[1]
            outs[0][:, side * cols : (side + 1) * cols] = value
        else:
            outs[side][0] = value


def paired_products(sides, joined=False):
    specs, operands = [], []

    def blocks(array, where):
        specs.append(pl.BlockSpec((1,) + array.shape[1:], lambda i: (listed(where, i), 0, 0)))
        operands.append(array)

    shared = sides[0][0] is sides[1][0] and sides[0][3][0] == sides[1][3][0]
    for side, (inputs, grads, arrived, at) in enumerate(sides):
        if side == 0 or not shared:
            blocks(inputs, at[0])
        specs.append(pl.BlockSpec(grads.shape, lambda i: (0, 0)))
        operands.append(grads)
        for array, where in zip(arrived, at[1:]):
            blocks(array, where)
    inputs, grads, arrived, at = sides[0]
    count, width, cols = len(at[0]), inputs.shape[1], grads.shape[1]
    if joined:
        out_specs = pl.BlockSpec((width, 2 * cols), lambda i: (0, 0))
        out_shape = jax.ShapeDtypeStruct((width, 2 * cols), jnp.bfloat16)
    else:
        out_specs = [pl.BlockSpec((1, width, cols), lambda i: (i, 0, 0))] * 2
        out_shape = [jax.ShapeDtypeStruct((count, width, cols), jnp.bfloat16)] * 2
    return pl.pallas_call(
        functools.partial(paired_kernel, len(arrived), shared, joined),
        grid=(count,),
        in_specs=specs,
        out_specs=out_specs,
        out_shape=out_shape,
        compiler_params=pltpu.CompilerParams(vmem_limit_bytes=VMEM_BYTES),
        name="projection_products",
    )(*operands)


def term_kernel(sets, *refs):
    dq_refs, refs = refs[:sets], refs[sets:]
    parts, refs = refs[: 3 * sets], refs[3 * sets :]
    wq_ref, wk_ref, wv_ref, out_ref, dk_ref, dv_ref = refs

    @pl.when(pl.program_id(0) == 0)
    def _():
        for c in range(sets):
            own_ref, one_ref, two_ref = parts[3 * c : 3 * c + 3]
            cols = own_ref.shape[2]
            at = slice(c * cols, (c + 1) * cols)
            for which, total_ref in enumerate((dk_ref, dv_ref)):
                total = own_ref[which] + one_ref[which].astype(jnp.float32)
                total = total + two_ref[which].astype(jnp.float32)
                total_ref[:, at] = total.astype(jnp.bfloat16)

    value = dot(wk_ref[...], dk_ref[...], NT) + dot(wv_ref[...], dv_ref[...], NT)
    for c, dq_ref in enumerate(dq_refs):
        cols = dq_ref.shape[1]
        value = value + dot(wq_ref[:, c * cols : (c + 1) * cols], dq_ref[...], NT)
    out_ref[0] = value.astype(jnp.bfloat16)


def input_term(dqs, halos, w_query, w_key, w_value, parts):
    sets, rows = len(dqs), dqs[0].shape[0]
    width = w_query.shape[0] // parts
    whole = [*dqs, *(part for halo in halos for part in halo)]
    weights = (w_query, w_key, w_value)
    key_cols = w_key.shape[1]

    def constant(array):
        return pl.BlockSpec(array.shape, lambda p: (0,) * array.ndim)

    total = jax.ShapeDtypeStruct((rows, key_cols), jnp.bfloat16)
    return pl.pallas_call(
        functools.partial(term_kernel, sets),
        grid=(parts,),
        in_specs=[constant(a) for a in whole]
        + [pl.BlockSpec((width, w.shape[1]), lambda p: (p, 0)) for w in weights],
        out_specs=[pl.BlockSpec((1, width, rows), lambda p: (p, 0, 0)), constant(total), constant(total)],
        out_shape=[jax.ShapeDtypeStruct((parts, width, rows), jnp.bfloat16), total, total],
        compiler_params=pltpu.CompilerParams(vmem_limit_bytes=VMEM_BYTES),
        name="input_term",
    )(*whole, *weights)


def swapped(block, bit):
    size = lax.axis_size("seq")
    return lax.ppermute(block, "seq", [(i, i ^ bit) for i in range(size)])


def shifted(block, distance):
    size = lax.axis_size("seq")
    return lax.ppermute(
        block, "seq", [(i, i + distance) for i in range(size) if 0 <= i + distance < size]
    )


def gray(index):
    return index ^ (index >> 1)


class Order:
    def __init__(self):
        self.last = ()

    def after(self, *values):
        values, _ = lax.optimization_barrier((values, self.last))
        return values if len(values) > 1 else values[0]

    def did(self, value):
        self.last = value
        return value


class Scattered:
    def __init__(self, offsets, bits):
        self.offsets = offsets
        self.bits = [list(bits), list(bits[::-1])]
        self.alive = [list(offsets)] * 2
        self.held = [[list(offsets)], [list(offsets)]]

    def summed(self, leaving, inputs, grads, arrived, joined=False):
        sides = []
        for i in range(2):
            at = [[held.index(o) for o in leaving[i]] for held in self.held[i]]
            at.insert(0, [self.offsets.index(o) for o in leaving[i]])
            sides.append((inputs, grads[i], [a[i] for a in arrived], at))
        return paired_products(sides, joined)

    def leaving(self, inputs, grads, arrived):
        leaving = [[o for o in self.alive[i] if o & self.bits[i][0]] for i in range(2)]
        return self.summed(leaving, inputs, grads, arrived)

    def step(self, blocks):
        bits = [b.pop(0) for b in self.bits]
        for i in range(2):
            self.held[i].append([o ^ bits[i] for o in self.alive[i] if o & bits[i]])
            self.alive[i] = [o for o in self.alive[i] if not o & bits[i]]
        return [swapped(block, bit) for block, bit in zip(blocks, bits)]

    def result(self, inputs, grads, arrived, joined=False):
        out = self.summed([[0], [0]], inputs, grads, arrived, joined)
        return out if joined else [o[0] for o in out]


def beside_products(odds, first, second):
    at = [list(range(odds.shape[0]))]
    blocks = paired_products([(odds, first, [], at), (odds, second, [], at)])
    return [swapped(block, 1) for block in blocks]


def kept_together(always, work, *operands):
    shapes = []

    def traced(*operands):
        out = work(*operands)
        shapes.append(jax.tree.map(lambda a: jax.ShapeDtypeStruct(a.shape, a.dtype), out))
        return out

    def nothing(*operands):
        return jax.tree.map(lambda a: jnp.zeros(a.shape, a.dtype), shapes[0])

    return lax.cond(always, traced, nothing, *operands)


def on_device(layer_input, query, keys, values, out_grad, w_query, w_key, w_value, proof_lengths):
    rows = query.shape[0]
    key_cols = keys.shape[1]
    kv_local = key_cols // HD
    groups = query.shape[1] // key_cols
    seq_size = lax.axis_size("seq")
    head_size = lax.axis_size("head")
    me = lax.axis_index("seq")
    odd = me % 2 == 1
    first_row = me * rows

    positions = first_row + jnp.arange(rows, dtype=jnp.int32)
    starts = jnp.cumsum(proof_lengths) - proof_lengths
    begun = starts[:, None] <= positions[None, :]
    proof_start = jnp.max(jnp.where(begun, starts[:, None], 0), axis=0)
    lowest = jnp.maximum(proof_start, positions - (WINDOW - 1)) - first_row + WINDOW
    lowest = lowest.astype(jnp.int32)[None, :]

    order = Order()
    sets = 2 if kv_local % 2 == 0 else 1
    per_set = kv_local // sets
    cols = per_set * HD

    def pair(c):
        at = slice(c * cols, (c + 1) * cols)
        return jnp.stack([keys[:, at], values[:, at]])

    own = order.did(pair(0))
    two_back = shifted(own, 2)
    steps = seq_size.bit_length() - 1
    even = [2 * gray(i) for i in range(1, seq_size // 2)] + [0]
    offsets = [o ^ 1 for o in even] + even
    layer_input = order.after(layer_input)
    odds, evens = order.did(arranged(layer_input, me, offsets))
    pieces = []
    for c in range(1, sets):
        keys, values = order.after(keys, values)
        other = order.did(pair(c))
        pieces.append([shifted(other, 2), shifted(other, 1), other])
    two_back = order.after(two_back)
    passed = order.did(jnp.where(odd, two_back, own))
    pieces.insert(0, [two_back, swapped(passed, 1), own])
    dqs, halos = [], []
    for c in range(sets):
        seen = order.after(*pieces[c])
        dq, halo_two, halo_one, own_grad = order.did(
            attention(lowest, query, out_grad, seen, c * per_set, groups)
        )
        dqs.append(dq)
        if c < sets - 1:
            halos.append((own_grad, shifted(halo_one, -1), shifted(halo_two, -2)))
    if sets == 2:
        halves = dqs
    else:
        half = dqs[0].shape[1] // 2
        halves = [dqs[0][:, :half], dqs[0][:, half:]]

    always = proof_lengths[0] > 0
    bits = [1 << j for j in range(1, steps)]
    query_sum, other_sum = Scattered(even, bits), Scattered(even, bits)

    def first_products(odds, evens, *dqs):
        beside = beside_products(odds, *dqs)
        return beside, query_sum.leaving(evens, dqs, [beside])

    def last_halo(halo_one, halo_two, *args):
        order = Order()
        arrived = shifted(halo_one, -1), shifted(halo_two, -2)
        products = order.did(kept_together(always, first_products, *args))
        return order.after(*arrived), products

    *args, early = order.after(halo_one, halo_two, odds, evens, *halves, [two for _, _, two in halos])
    halos = [(own, one, two) for (own, one, _), two in zip(halos, early)]
    arrived, (beside, blocks) = order.did(kept_together(always, last_halo, *args))
    halos.append((own_grad, *arrived))
    dqs, halos = order.after(dqs, halos)
    term, dk, dv = order.did(input_term(dqs, halos, w_query, w_key, w_value, head_size))

    def projections(odds, evens, dqs, beside, blocks, dk, dv):
        order = Order()
        arrived = [beside, query_sum.step(blocks)]
        args = order.after(odds, dk, dv)
        beside = order.did(kept_together(always, beside_products, *args))
        others = order.did(other_sum.leaving(evens, [dk, dv], [beside]))
        other_arrived = [beside, other_sum.step(others)]
        while query_sum.bits[0]:
            held = order.after(arrived)
            blocks = order.did(query_sum.leaving(evens, dqs, held))
            arrived = arrived + [query_sum.step(blocks)]
            held = order.after(other_arrived)
            blocks = order.did(other_sum.leaving(evens, [dk, dv], held))
            other_arrived = other_arrived + [other_sum.step(blocks)]
        held = order.after(arrived)
        wq_grad = order.did(query_sum.result(evens, dqs, held, True))
        held = order.after(other_arrived)
        return (wq_grad, *other_sum.result(evens, [dk, dv], held))

    def finish(term, *args):
        grads = kept_together(always, projections, *args)
        total = lax.psum_scatter(term, "head", scatter_dimension=0, tiled=False)
        return (total, *grads)

    args = order.after(odds, evens, halves, beside, blocks, dk, dv)
    input_grad, *grads = finish(term, *args)
    return (input_grad.T, *grads)


def solution(mesh):
    return jax.shard_map(
        on_device,
        mesh=mesh,
        in_specs=(
            P("seq", None),
            P("seq", "head"),
            P("seq", "head"),
            P("seq", "head"),
            P("seq", "head"),
            P(None, "head"),
            P(None, "head"),
            P(None, "head"),
            P(),
        ),
        out_specs=(P("seq", "head"), P("seq", "head"), P("seq", "head"), P("seq", "head")),
        check_vma=False,
    )
```

```python
import functools
import math

import jax
import jax.numpy as jnp
from jax import lax
from jax.experimental import pallas as pl
from jax.experimental.pallas import tpu as pltpu
from jax.sharding import PartitionSpec as P

D = 5376
H = 32
HD = 128
WINDOW = 1024
TILE = 256
SCALE = (D // H) ** (-0.5)
FAR = -1e30
VMEM_BYTES = 40 * 1024 * 1024

NT = (((1,), (1,)), ((), ()))
TN = (((0,), (0,)), ((), ()))


def dot(left, right, dims=(((1,), (0,)), ((), ()))):
    return lax.dot_general(left, right, dims, preferred_element_type=jnp.float32)


def attention_kernel(groups, depth, lowest_ref, q_ref, g_ref, *refs):
    pieces = refs[: depth + 1]
    dq_ref = refs[depth + 1]
    halo_refs = refs[depth + 2 : 2 * depth + 2]
    own_ref = refs[2 * depth + 2]
    score_scr, pgrad_scr, dk_scr, dv_scr = refs[2 * depth + 3 :]
    rows = q_ref.shape[0]
    per_piece = rows // TILE
    behind = WINDOW // TILE
    lanes = groups * TILE

    def key_tile(e, which):
        start = (e % per_piece) * TILE
        return pieces[e // per_piece][which, start : start + TILE, :]

    key_iota = lax.broadcasted_iota(jnp.int32, (TILE, 1), 0)
    query_iota = lax.broadcasted_iota(jnp.int32, (1, TILE), 1)
    query_iota = jnp.concatenate([query_iota] * groups, axis=1)
    factor = SCALE * math.log2(math.e)

    def scores(t):
        here = slice(t * TILE, (t + 1) * TILE)
        q2 = jnp.concatenate([q_ref[here, j * HD : (j + 1) * HD] for j in range(groups)], axis=0)
        g2 = jnp.concatenate([g_ref[here, j * HD : (j + 1) * HD] for j in range(groups)], axis=0)
        lowest = jnp.concatenate([lowest_ref[:, here]] * groups, axis=1)
        top = jnp.full((1, lanes), FAR, jnp.float32)
        for b in range(behind + 1):
            s = dot(key_tile(t + b, 0), q2, NT)
            allowed = key_iota + (t + b) * TILE >= lowest
            if b == behind:
                allowed = allowed & (key_iota <= query_iota)
            s = jnp.where(allowed, s, FAR)
            score_scr[t % 2, b * TILE : (b + 1) * TILE, :] = s
            top = jnp.maximum(top, jnp.max(s, axis=0, keepdims=True))
        return q2, g2, top

    def weights(t, q2, g2, top):
        total = jnp.zeros((1, lanes), jnp.float32)
        delta = jnp.zeros((1, lanes), jnp.float32)
        for b in range(behind + 1):
            at = slice(b * TILE, (b + 1) * TILE)
            weight = jnp.exp2((score_scr[t % 2, at, :] - top) * factor)
            pgrad = dot(key_tile(t + b, 1), g2, NT)
            score_scr[t % 2, at, :] = weight
            pgrad_scr[t % 2, at, :] = pgrad
            total = total + jnp.sum(weight, axis=0, keepdims=True)
            delta = delta + jnp.sum(weight * pgrad, axis=0, keepdims=True)
        inverse = 1.0 / total
        return q2, g2, inverse, delta * inverse

    def grads(t, q2, g2, inverse, delta):
        here = slice(t * TILE, (t + 1) * TILE)
        dq = jnp.zeros((HD, lanes), jnp.float32)
        for b in range(behind + 1):
            at = slice(b * TILE, (b + 1) * TILE)
            e = t + b
            to = slice(e * TILE, (e + 1) * TILE)
            prob = score_scr[t % 2, at, :] * inverse
            sgrad = (prob * (pgrad_scr[t % 2, at, :] - delta)).astype(jnp.bfloat16)
            dv = dot(prob.astype(jnp.bfloat16), g2)
            dk = dot(sgrad, q2)
            if t == 0 or b == behind:
                dv_scr[to, :] = dv
                dk_scr[to, :] = dk
            else:
                dv_scr[to, :] += dv
                dk_scr[to, :] += dk
            dq = dq + dot(key_tile(e, 0), sgrad, TN)
        dq = (dq * SCALE).T.astype(jnp.bfloat16)
        for j in range(groups):
            dq_ref[here, j * HD : (j + 1) * HD] = dq[j * TILE : (j + 1) * TILE, :]

    held = scores(0)
    for t in range(per_piece):
        held = weights(t, *held)
        later = scores(t + 1) if t + 1 < per_piece else None
        grads(t, *held)
        held = later
    for d in range(depth):
        at = slice(d * rows, (d + 1) * rows)
        halo_refs[d][0] = (dk_scr[at, :] * SCALE).astype(jnp.bfloat16)
        halo_refs[d][1] = dv_scr[at, :].astype(jnp.bfloat16)
    own_ref[0] = dk_scr[depth * rows :, :] * SCALE
    own_ref[1] = dv_scr[depth * rows :, :]


def attention(lowest, query, out_grad, pieces, first, groups):
    rows = query.shape[0]
    depth = len(pieces) - 1
    heads = pieces[0].shape[2] // HD
    wide = groups * HD
    query_spec = pl.BlockSpec((rows, wide), lambda h: (0, h + first))
    pair_spec = pl.BlockSpec((2, rows, HD), lambda h: (0, 0, h))
    span = WINDOW + TILE
    pair = jax.ShapeDtypeStruct((2, rows, heads * HD), jnp.bfloat16)
    return pl.pallas_call(
        functools.partial(attention_kernel, groups, depth),
        grid=(heads,),
        in_specs=[pl.BlockSpec((1, rows), lambda h: (0, 0)), query_spec, query_spec]
        + [pair_spec] * (depth + 1),
        out_specs=[pl.BlockSpec((rows, wide), lambda h: (0, h))] + [pair_spec] * (depth + 1),
        out_shape=[jax.ShapeDtypeStruct((rows, heads * wide), jnp.bfloat16)]
        + [pair] * depth
        + [jax.ShapeDtypeStruct(pair.shape, jnp.float32)],
        scratch_shapes=[
            pltpu.VMEM((2, span, groups * TILE), jnp.float32),
            pltpu.VMEM((2, span, groups * TILE), jnp.float32),
            pltpu.VMEM((WINDOW + rows, HD), jnp.float32),
            pltpu.VMEM((WINDOW + rows, HD), jnp.float32),
        ],
        compiler_params=pltpu.CompilerParams(vmem_limit_bytes=VMEM_BYTES),
        name="attention_grads",
    )(lowest, query, out_grad, *pieces)


def arrange_kernel(offsets, me_ref, x_ref, first_ref, second_ref, scratch):
    width = first_ref.shape[1]
    step = pl.program_id(0)
    half = pl.num_programs(0) // 2

    @pl.when(step == 0)
    def _():
        tile = 768 if x_ref.shape[1] % 768 == 0 else 128
        for i in range(x_ref.shape[1] // tile):
            at = slice(i * tile, (i + 1) * tile)
            scratch[at, :] = x_ref[:, at].T

    start = pl.multiple_of((listed(offsets, step) ^ me_ref[0]) * width, 16)

    @pl.when(step < half)
    def _():
        first_ref[0] = scratch[pl.ds(start, width), :]

    @pl.when(step >= half)
    def _():
        second_ref[0] = scratch[pl.ds(start, width), :]


def arranged(array, me, offsets):
    rows, cols = array.shape
    count = len(offsets)
    width, half = cols // count, count // 2
    out = jax.ShapeDtypeStruct((half, width, rows), array.dtype)
    return pl.pallas_call(
        functools.partial(arrange_kernel, offsets),
        grid_spec=pltpu.PrefetchScalarGridSpec(
            num_scalar_prefetch=1,
            grid=(count,),
            in_specs=[pl.BlockSpec((rows, cols), lambda i, me_ref: (0, 0))],
            out_specs=[
                pl.BlockSpec((1, width, rows), lambda i, me_ref: (jnp.minimum(i, half - 1), 0, 0)),
                pl.BlockSpec((1, width, rows), lambda i, me_ref: (jnp.maximum(i - half, 0), 0, 0)),
            ],
            scratch_shapes=[pltpu.VMEM((cols, rows), array.dtype)],
        ),
        out_shape=[out, out],
        compiler_params=pltpu.CompilerParams(vmem_limit_bytes=VMEM_BYTES),
        name="arranged_input",
    )(me.reshape(1), array)


def listed(values, index):
    total = jnp.int32(values[0])
    for i, value in enumerate(values[1:], 1):
        total = jnp.where(index == i, jnp.int32(value), total)
    return total


def paired_kernel(count, shared, joined, *refs):
    sides = 2 * [refs[:1]] if shared else [refs[:1], refs[2 + count : 3 + count]]
    sides = [(*x, *refs[i * (1 + count) + (1 if shared else i + 1) :][: 1 + count]) for i, x in enumerate(sides)]
    outs = refs[2 * (1 + count) + (1 if shared else 2) :]
    for side in range(2):
        x_ref, g_ref, *arrived = sides[side]
        value = dot(x_ref[0], g_ref[...])
        for ref in arrived:
            value = value + ref[0].astype(jnp.float32)
        value = value.astype(jnp.bfloat16)
        if joined:
            cols = value.shape[1]
            outs[0][:, side * cols : (side + 1) * cols] = value
        else:
            outs[side][0] = value


def paired_products(sides, joined=False):
    specs, operands = [], []

    def blocks(array, where):
        specs.append(pl.BlockSpec((1,) + array.shape[1:], lambda i: (listed(where, i), 0, 0)))
        operands.append(array)

    shared = sides[0][0] is sides[1][0] and sides[0][3][0] == sides[1][3][0]
    for side, (inputs, grads, arrived, at) in enumerate(sides):
        if side == 0 or not shared:
            blocks(inputs, at[0])
        specs.append(pl.BlockSpec(grads.shape, lambda i: (0, 0)))
        operands.append(grads)
        for array, where in zip(arrived, at[1:]):
            blocks(array, where)
    inputs, grads, arrived, at = sides[0]
    count, width, cols = len(at[0]), inputs.shape[1], grads.shape[1]
    if joined:
        out_specs = pl.BlockSpec((width, 2 * cols), lambda i: (0, 0))
        out_shape = jax.ShapeDtypeStruct((width, 2 * cols), jnp.bfloat16)
    else:
        out_specs = [pl.BlockSpec((1, width, cols), lambda i: (i, 0, 0))] * 2
        out_shape = [jax.ShapeDtypeStruct((count, width, cols), jnp.bfloat16)] * 2
    return pl.pallas_call(
        functools.partial(paired_kernel, len(arrived), shared, joined),
        grid=(count,),
        in_specs=specs,
        out_specs=out_specs,
        out_shape=out_shape,
        compiler_params=pltpu.CompilerParams(vmem_limit_bytes=VMEM_BYTES),
        name="projection_products",
    )(*operands)


def term_kernel(sets, *refs):
    dq_refs, refs = refs[:sets], refs[sets:]
    parts, refs = refs[: 3 * sets], refs[3 * sets :]
    wq_ref, wk_ref, wv_ref, out_ref, dk_ref, dv_ref = refs

    @pl.when(pl.program_id(0) == 0)
    def _():
        for c in range(sets):
            own_ref, one_ref, two_ref = parts[3 * c : 3 * c + 3]
            cols = own_ref.shape[2]
            at = slice(c * cols, (c + 1) * cols)
            for which, total_ref in enumerate((dk_ref, dv_ref)):
                total = own_ref[which] + one_ref[which].astype(jnp.float32)
                total = total + two_ref[which].astype(jnp.float32)
                total_ref[:, at] = total.astype(jnp.bfloat16)

    value = dot(wk_ref[...], dk_ref[...], NT) + dot(wv_ref[...], dv_ref[...], NT)
    for c, dq_ref in enumerate(dq_refs):
        cols = dq_ref.shape[1]
        value = value + dot(wq_ref[:, c * cols : (c + 1) * cols], dq_ref[...], NT)
    out_ref[0] = value.astype(jnp.bfloat16)


def input_term(dqs, halos, w_query, w_key, w_value, parts):
    sets, rows = len(dqs), dqs[0].shape[0]
    width = w_query.shape[0] // parts
    whole = [*dqs, *(part for halo in halos for part in halo)]
    weights = (w_query, w_key, w_value)
    key_cols = w_key.shape[1]

    def constant(array):
        return pl.BlockSpec(array.shape, lambda p: (0,) * array.ndim)

    total = jax.ShapeDtypeStruct((rows, key_cols), jnp.bfloat16)
    return pl.pallas_call(
        functools.partial(term_kernel, sets),
        grid=(parts,),
        in_specs=[constant(a) for a in whole]
        + [pl.BlockSpec((width, w.shape[1]), lambda p: (p, 0)) for w in weights],
        out_specs=[pl.BlockSpec((1, width, rows), lambda p: (p, 0, 0)), constant(total), constant(total)],
        out_shape=[jax.ShapeDtypeStruct((parts, width, rows), jnp.bfloat16), total, total],
        compiler_params=pltpu.CompilerParams(vmem_limit_bytes=VMEM_BYTES),
        name="input_term",
    )(*whole, *weights)


def swapped(block, bit):
    size = lax.axis_size("seq")
    return lax.ppermute(block, "seq", [(i, i ^ bit) for i in range(size)])


def shifted(block, distance):
    size = lax.axis_size("seq")
    return lax.ppermute(
        block, "seq", [(i, i + distance) for i in range(size) if 0 <= i + distance < size]
    )


def gray(index):
    return index ^ (index >> 1)


class Order:
    def __init__(self):
        self.last = ()

    def after(self, *values):
        values, _ = lax.optimization_barrier((values, self.last))
        return values if len(values) > 1 else values[0]

    def did(self, value):
        self.last = value
        return value


class Scattered:
    def __init__(self, offsets, bits):
        self.offsets = offsets
        self.bits = [list(bits), list(bits[::-1])]
        self.alive = [list(offsets)] * 2
        self.held = [[list(offsets)], [list(offsets)]]

    def summed(self, leaving, inputs, grads, arrived, joined=False):
        sides = []
        for i in range(2):
            at = [[held.index(o) for o in leaving[i]] for held in self.held[i]]
            at.insert(0, [self.offsets.index(o) for o in leaving[i]])
            sides.append((inputs, grads[i], [a[i] for a in arrived], at))
        return paired_products(sides, joined)

    def leaving(self, inputs, grads, arrived):
        leaving = [[o for o in self.alive[i] if o & self.bits[i][0]] for i in range(2)]
        return self.summed(leaving, inputs, grads, arrived)

    def step(self, blocks):
        bits = [b.pop(0) for b in self.bits]
        for i in range(2):
            self.held[i].append([o ^ bits[i] for o in self.alive[i] if o & bits[i]])
            self.alive[i] = [o for o in self.alive[i] if not o & bits[i]]
        return [swapped(block, bit) for block, bit in zip(blocks, bits)]

    def result(self, inputs, grads, arrived, joined=False):
        out = self.summed([[0], [0]], inputs, grads, arrived, joined)
        return out if joined else [o[0] for o in out]


def beside_products(odds, first, second):
    at = [list(range(odds.shape[0]))]
    blocks = paired_products([(odds, first, [], at), (odds, second, [], at)])
    return [swapped(block, 1) for block in blocks]


def kept_together(always, work, *operands):
    shapes = []

    def traced(*operands):
        out = work(*operands)
        shapes.append(jax.tree.map(lambda a: jax.ShapeDtypeStruct(a.shape, a.dtype), out))
        return out

    def nothing(*operands):
        return jax.tree.map(lambda a: jnp.zeros(a.shape, a.dtype), shapes[0])

    return lax.cond(always, traced, nothing, *operands)


def on_device(layer_input, query, keys, values, out_grad, w_query, w_key, w_value, proof_lengths):
    rows = query.shape[0]
    key_cols = keys.shape[1]
    kv_local = key_cols // HD
    groups = query.shape[1] // key_cols
    seq_size = lax.axis_size("seq")
    head_size = lax.axis_size("head")
    me = lax.axis_index("seq")
    odd = me % 2 == 1
    first_row = me * rows

    positions = first_row + jnp.arange(rows, dtype=jnp.int32)
    starts = jnp.cumsum(proof_lengths) - proof_lengths
    begun = starts[:, None] <= positions[None, :]
    proof_start = jnp.max(jnp.where(begun, starts[:, None], 0), axis=0)
    lowest = jnp.maximum(proof_start, positions - (WINDOW - 1)) - first_row + WINDOW
    lowest = lowest.astype(jnp.int32)[None, :]

    order = Order()
    sets = 2 if kv_local % 2 == 0 else 1
    per_set = kv_local // sets
    cols = per_set * HD

    def pair(c):
        at = slice(c * cols, (c + 1) * cols)
        return jnp.stack([keys[:, at], values[:, at]])

    own = order.did(pair(0))
    two_back = shifted(own, 2)
    steps = seq_size.bit_length() - 1
    even = [2 * gray(i) for i in range(1, seq_size // 2)] + [0]
    offsets = [o ^ 1 for o in even] + even
    layer_input = order.after(layer_input)
    odds, evens = order.did(arranged(layer_input, me, offsets))
    pieces = []
    for c in range(1, sets):
        keys, values = order.after(keys, values)
        other = order.did(pair(c))
        pieces.append([shifted(other, 2), shifted(other, 1), other])
    two_back = order.after(two_back)
    passed = order.did(jnp.where(odd, two_back, own))
    pieces.insert(0, [two_back, swapped(passed, 1), own])
    dqs, halos = [], []
    for c in range(sets):
        seen = order.after(*pieces[c])
        dq, halo_two, halo_one, own_grad = order.did(
            attention(lowest, query, out_grad, seen, c * per_set, groups)
        )
        dqs.append(dq)
        if c < sets - 1:
            halos.append((own_grad, shifted(halo_one, -1), shifted(halo_two, -2)))
    if sets == 2:
        halves = dqs
    else:
        half = dqs[0].shape[1] // 2
        halves = [dqs[0][:, :half], dqs[0][:, half:]]

    always = proof_lengths[0] > 0
    bits = [1 << j for j in range(1, steps)]
    query_sum, other_sum = Scattered(even, bits), Scattered(even, bits)

    def first_products(odds, evens, *dqs):
        beside = beside_products(odds, *dqs)
        return beside, query_sum.leaving(evens, dqs, [beside])

    def last_halo(halo_one, halo_two, *args):
        order = Order()
        arrived = shifted(halo_one, -1), shifted(halo_two, -2)
        products = order.did(kept_together(always, first_products, *args))
        return order.after(*arrived), products

    *args, early = order.after(halo_one, halo_two, odds, evens, *halves, [two for _, _, two in halos])
    halos = [(own, one, two) for (own, one, _), two in zip(halos, early)]
    arrived, (beside, blocks) = order.did(kept_together(always, last_halo, *args))
    halos.append((own_grad, *arrived))
    dqs, halos = order.after(dqs, halos)
    term, dk, dv = order.did(input_term(dqs, halos, w_query, w_key, w_value, head_size))

    def projections(odds, evens, dqs, beside, blocks, dk, dv):
        order = Order()
        arrived = [beside, query_sum.step(blocks)]
        args = order.after(odds, dk, dv)
        beside = order.did(kept_together(always, beside_products, *args))
        others = order.did(other_sum.leaving(evens, [dk, dv], [beside]))
        other_arrived = [beside, other_sum.step(others)]
        while query_sum.bits[0]:
            held = order.after(arrived)
            blocks = order.did(query_sum.leaving(evens, dqs, held))
            arrived = arrived + [query_sum.step(blocks)]
            held = order.after(other_arrived)
            blocks = order.did(other_sum.leaving(evens, [dk, dv], held))
            other_arrived = other_arrived + [other_sum.step(blocks)]
        held = order.after(arrived)
        wq_grad = order.did(query_sum.result(evens, dqs, held, True))
        held = order.after(other_arrived)
        return (wq_grad, *other_sum.result(evens, [dk, dv], held))

    def finish(term, *args):
        grads = kept_together(always, projections, *args)
        total = lax.psum_scatter(term, "head", scatter_dimension=0, tiled=False)
        return (total, *grads)

    args = order.after(odds, evens, halves, beside, blocks, dk, dv)
    input_grad, *grads = finish(term, *args)
    return (input_grad.T, *grads)


def solution(mesh):
    return jax.shard_map(
        on_device,
        mesh=mesh,
        in_specs=(
            P("seq", None),
            P("seq", "head"),
            P("seq", "head"),
            P("seq", "head"),
            P("seq", "head"),
            P(None, "head"),
            P(None, "head"),
            P(None, "head"),
            P(),
        ),
        out_specs=(P("seq", "head"), P("seq", "head"), P("seq", "head"), P("seq", "head")),
        check_vma=False,
    )
```
